256 devices in a mesh: rows: 32 (over x_hi, z, core), cols: 8 (over x_lo, y).
Axes of the slice: x: 4 (x_hi: 2, x_lo: 2; x = x_hi * 2 + x_lo), y: 4, z: 8, core: 2. Of those that a mesh axis runs over, the one named last changes fastest.
Arguments:
- object_field: float32 [2, 16384, 4096], P(None, 'rows', 'cols'), may hold values from -6 to 6
- probe: float32 [4, 2, 256, 256], replicated, may hold values from -6 to 6
- photons: int32 [32, 8, 4, 256, 256], P('rows', 'cols'), may hold values from 0 to 40
- positions: int32 [32, 8, 4, 2], P('rows', 'cols'), may hold values from -128 to 384
- live_counts: int32 [32, 8], P('rows', 'cols'), may hold values from 1 to 4, as said below
Outputs:
- object_grad: float32 [2, 16384, 4096], P(None, 'rows', 'cols')
- probe_grad: float32 [4, 2, 256, 256], replicated
The draws below stay inside these ranges and needn't reach their ends.
Inputs may be any that keep to these rules, and one draw needn't show every extreme that they name: `live_counts`: some tile has 4 live slots in every draw.
All inputs are finite; a program needn't handle non-finite values.
Results may differ from the reference program's by a relative error of at most 0.0039.
The reference program's roundings to bfloat16 on the way count: a program that leaves them out, or rounds other values in their place, can miss the bound.
Values sent between devices are 32-bit elements; how exact they have to be, the bound alone decides.
A program may use at most 64 MiB of HBM per device.

```python
import math
import jax
import jax.numpy as jnp
from jax import lax

PROBE = 256
MODES = 4
HALO = 128
TILE = 512
POS_DEV = 4
NROW = 16384
NCOL = 4096
N_ROWS = 32
N_COLS = 8


def draw_live_counts(key, part):
    key = jax.random.fold_in(key, 7)
    key_full, key_small = jax.random.split(key)
    heavy = jax.random.randint(key_full, (N_ROWS, N_COLS), 0, 4) == 0
    light = jax.random.randint(key_small, (N_ROWS, N_COLS), 1, max(POS_DEV // 2, 1) + 1)
    counts = jnp.where(heavy, POS_DEV, light).astype(jnp.int32)
    return counts.at[0, 0].set(POS_DEV)


def place_ends(result, rng, low, top_value):
    shape = result.shape
    index_at = [jax.random.randint(jax.random.fold_in(rng, axis), (), 0, shape[axis]) for axis in range(len(shape))]
    result = result.at[tuple(index_at)].set(low)
    longest = shape.index(max(shape))
    index_at[longest] = (index_at[longest] + 1) % shape[longest]
    return result.at[tuple(index_at)].set(top_value)


def levels(key, extent, pieces, smallest, high):
    gain = 1.0
    for position, shards_of in pieces:
        draws = jax.random.uniform(jax.random.fold_in(jax.random.fold_in(key, 6), position), (shards_of,), jnp.float32, smallest / len(pieces), high / len(pieces))
        gain = gain * jnp.repeat(jnp.exp(draws), extent[position] // shards_of).reshape((-1,) + (1,) * (len(extent) - 1 - position))
    return gain


def scatter_about(stream_key, extent, deviation, bound, cuts=(), held_as=jnp.bfloat16):
    values = deviation * jax.random.normal(stream_key, extent, jnp.float32)
    if cuts:
        values = values * levels(stream_key, extent, cuts, -0.22, 0.18)
    return jnp.clip(values, -bound, bound).astype(held_as)


def setup_inputs(seed: int = 0) -> dict:
    arg_keys = jax.random.split(jax.random.key(seed), 6)
    return {
        "object_field": scatter_about(arg_keys[0], (2, NROW, NCOL), 1.0, 6.0, ((1, 32), (2, 8)), jnp.float32),
        "probe": scatter_about(arg_keys[1], (MODES, 2, PROBE, PROBE), 1.0, 6.0, (), jnp.float32),
        "photons": place_ends(jax.random.randint(arg_keys[2], (N_ROWS, N_COLS, POS_DEV, PROBE, PROBE), 0, 41), jax.random.fold_in(arg_keys[2], 1), 0, 40).astype(jnp.int32),
        "positions": place_ends(jax.random.randint(arg_keys[3], (N_ROWS, N_COLS, POS_DEV, 2), 0 - HALO, TILE + HALO - PROBE + 1), jax.random.fold_in(arg_keys[3], 1), 0 - HALO, TILE + HALO - PROBE).astype(jnp.int32),
        "live_counts": draw_live_counts(jax.random.fold_in(arg_keys[5], 71), 0),
    }


background = 1.0

def dft_tables(wave_size):
    ramp = jnp.arange(wave_size, dtype=jnp.int32)
    phases = ramp[:, None] * ramp[None, :] % wave_size
    angles = phases.astype(jnp.float32) * (2.0 * math.pi / wave_size)
    scaling = 1.0 / math.sqrt(wave_size)
    return ((jnp.cos(angles) * scaling).astype(jnp.bfloat16), (jnp.sin(angles) * scaling).astype(jnp.bfloat16))

def batch_left(table, values):
    return jnp.einsum('ab,mbc->mac', table.astype(jnp.float32), values.astype(jnp.float32), precision=lax.Precision.HIGHEST)

def batch_right(values, table):
    return jnp.einsum('mab,bc->mac', values.astype(jnp.float32), table.astype(jnp.float32), precision=lax.Precision.HIGHEST)

def left_apply(cos_t, sin_t, part_re, part_im, orient):
    out_re = batch_left(cos_t, part_re) - orient * batch_left(sin_t, part_im)
    out_im = batch_left(cos_t, part_im) + orient * batch_left(sin_t, part_re)
    return (out_re, out_im)

def right_apply(cos_t, sin_t, part_re, part_im, orient):
    out_re = batch_right(part_re, cos_t) - orient * batch_right(part_im, sin_t)
    out_im = batch_right(part_im, cos_t) + orient * batch_right(part_re, sin_t)
    return (out_re, out_im)

def slot_terms(patch, counts_here, probe, cos_t, sin_t):
    probe_re, probe_im = (probe[:, 0], probe[:, 1])
    patch_re, patch_im = (patch[0], patch[1])
    exit_re = (probe_re * patch_re - probe_im * patch_im).astype(jnp.bfloat16)
    exit_im = (probe_re * patch_im + probe_im * patch_re).astype(jnp.bfloat16)
    half_re, half_im = left_apply(cos_t, sin_t, exit_re, exit_im, -1.0)
    wave_re, wave_im = right_apply(cos_t, sin_t, half_re.astype(jnp.bfloat16), half_im.astype(jnp.bfloat16), -1.0)
    intensity = lax.optimization_barrier(jnp.sum(wave_re * wave_re + wave_im * wave_im, axis=0)) + background
    factor = 1.0 - counts_here.astype(jnp.float32) / intensity
    update_re = (factor * wave_re).astype(jnp.bfloat16)
    update_im = (factor * wave_im).astype(jnp.bfloat16)
    back_re, back_im = left_apply(cos_t, sin_t, update_re, update_im, 1.0)
    chi_re, chi_im = right_apply(cos_t, sin_t, back_re.astype(jnp.bfloat16), back_im.astype(jnp.bfloat16), 1.0)
    object_term = jnp.stack([lax.optimization_barrier(jnp.sum(probe_re * chi_re + probe_im * chi_im, axis=0)), lax.optimization_barrier(jnp.sum(probe_re * chi_im - probe_im * chi_re, axis=0))])
    probe_term = jnp.stack([patch_re * chi_re + patch_im * chi_im, patch_re * chi_im - patch_im * chi_re], axis=1)
    return (object_term, probe_term)

def reference(object_field, probe, photons, positions, live_counts):
    rim_width = PROBE // 2
    cos_t, sin_t = dft_tables(PROBE)
    padded = jnp.pad(object_field, ((0, 0), (rim_width, rim_width), (rim_width, rim_width)))
    slot_count = N_ROWS * N_COLS * POS_DEV
    flat_pos = positions.reshape(slot_count, 2)
    flat_counts = photons.reshape(slot_count, PROBE, PROBE)
    slot_ids = jnp.arange(slot_count, dtype=jnp.int32)
    device_id = slot_ids // POS_DEV
    slot_rank = slot_ids % POS_DEV
    row_id = device_id // N_COLS
    col_id = device_id % N_COLS
    is_live = slot_rank < live_counts.reshape(-1)[device_id]
    row_start = (row_id * TILE + flat_pos[:, 0] + rim_width).astype(jnp.int32)
    col_start = (col_id * TILE + flat_pos[:, 1] + rim_width).astype(jnp.int32)
    anchor = jnp.int32(0)

    def advance(running, element):
        top_row, left_col, counts_here, alive_flag = element

        def process(state):
            gradient, probe_acc = state
            patch = lax.dynamic_slice(padded, (anchor, top_row, left_col), (2, PROBE, PROBE))
            object_term, probe_term = slot_terms(patch, counts_here, probe, cos_t, sin_t)
            before = lax.dynamic_slice(gradient, (anchor, top_row, left_col), (2, PROBE, PROBE))
            gradient = lax.dynamic_update_slice(gradient, before + object_term, (anchor, top_row, left_col))
            return (gradient, probe_acc + probe_term)

        def unchanged(state):
            return state
        return (lax.cond(alive_flag, process, unchanged, running), None)
    start_state = (jnp.zeros(padded.shape, jnp.float32), jnp.zeros(probe.shape, jnp.float32))
    (gradient, probe_acc), _ = lax.scan(advance, start_state, (row_start, col_start, flat_counts, is_live))
    object_grad = gradient[:, rim_width:-rim_width, rim_width:-rim_width]
    return (object_grad, probe_acc / math.sqrt(N_ROWS * N_COLS))
```

```python
import functools
import math

import jax
import jax.numpy as jnp
from jax import lax
from jax.experimental import pallas as pl
from jax.experimental.pallas import tpu as pltpu
from jax.sharding import PartitionSpec as P

MESH = pl.DeviceIdType.MESH
background = 1.0
S = 256
RIM = 128
T = 512
E = T + 2 * RIM
M = 4
SLOTS = 4
WROWS, WCOLS = S + 8, S + 128


def dft_table(wave_size):
    ramp = jnp.arange(wave_size, dtype=jnp.int32)
    phases = ramp[:, None] * ramp[None, :] % wave_size
    angles = phases.astype(jnp.float32) * (2.0 * math.pi / wave_size)
    scaling = 1.0 / math.sqrt(wave_size)
    cos_t = (jnp.cos(angles) * scaling).astype(jnp.bfloat16)
    sin_t = (jnp.sin(angles) * scaling).astype(jnp.bfloat16)
    return jnp.concatenate(
        [jnp.concatenate([cos_t, sin_t], axis=1), jnp.concatenate([-sin_t, cos_t], axis=1)], axis=0
    )


def halo_kernel(tile, out, padded, send_sem, recv_sem, own_sem, out_sem):
    r, c = lax.axis_index("rows"), lax.axis_index("cols")
    n_r, n_c = lax.axis_size("rows"), lax.axis_size("cols")
    up, down, left, right = r > 0, r < n_r - 1, c > 0, c < n_c - 1
    to_up, to_down, to_left, to_right = (r - 1, c), (r + 1, c), (r, c - 1), (r, c + 1)
    sides = ((up, to_up), (down, to_down), (left, to_left), (right, to_right))
    lo, mid, hi = pl.ds(0, RIM), pl.ds(RIM, T), pl.ds(RIM + T, RIM)

    center = padded.at[:, mid, mid]
    own = pltpu.make_async_copy(tile, center, own_sem)
    own.start()
    barrier = pltpu.get_barrier_semaphore()
    for there, device in sides:

        @pl.when(there)
        def _(device=device):
            pl.semaphore_signal(barrier, inc=1, device_id=device, device_id_type=MESH)

    own.wait()
    pl.semaphore_wait(barrier, sum(jnp.where(there, 1, 0) for there, _ in sides))

    def copy(index, src, dst, device):
        return pltpu.make_async_remote_copy(
            src_ref=src,
            dst_ref=dst,
            send_sem=send_sem.at[index],
            recv_sem=recv_sem.at[index],
            device_id=device,
            device_id_type=MESH,
        )

    near, far = pl.ds(RIM, RIM), pl.ds(T, RIM)
    spans = (pl.ds(RIM, RIM), pl.ds(T, RIM), pl.ds(2 * RIM, T - 2 * RIM))
    to_l = [copy(i, padded.at[:, spans[i], near], padded.at[:, spans[i], hi], to_left) for i in range(3)]
    to_r = [copy(3 + i, padded.at[:, spans[i], far], padded.at[:, spans[i], lo], to_right) for i in range(3)]
    to_u = copy(6, padded.at[:, near, mid], padded.at[:, hi, mid], to_up)
    to_d = copy(7, padded.at[:, far, mid], padded.at[:, lo, mid], to_down)
    c_ul = copy(8, padded.at[:, near, lo], padded.at[:, hi, lo], to_up)
    c_ur = copy(9, padded.at[:, near, hi], padded.at[:, hi, hi], to_up)
    c_dl = copy(10, padded.at[:, far, lo], padded.at[:, lo, lo], to_down)
    c_dr = copy(11, padded.at[:, far, hi], padded.at[:, lo, hi], to_down)

    def starts(there, *some):
        @pl.when(there)
        def _():
            for one in some:
                one.start()

    for i in range(3):
        starts(left, to_l[i])
        starts(right, to_r[i])
        if i == 0:
            starts(up, to_u)
            starts(down, to_d)

    stored = []

    def store(rows, cols):
        one = pltpu.make_async_copy(padded.at[:, rows, cols], out.at[:, rows, cols], out_sem.at[len(stored)])
        one.start()
        stored.append(one)

    def arrived(there, rows, cols, *some):
        @pl.when(there)
        def _():
            for one in some:
                one.wait_recv()

        @pl.when(jnp.logical_not(there))
        def _():
            padded[:, rows, cols] = jnp.zeros((2, rows.size, cols.size), jnp.float32)

    store(mid, mid)
    arrived(left, near, lo, to_r[0])
    starts(left & up, c_ul)
    arrived(right, near, hi, to_l[0])
    starts(right & up, c_ur)
    arrived(left, far, lo, to_r[1])
    starts(left & down, c_dl)
    arrived(right, far, hi, to_l[1])
    starts(right & down, c_dr)
    arrived(up, lo, mid, to_d)
    store(lo, mid)
    arrived(down, hi, mid, to_u)
    store(hi, mid)
    arrived(up & left, lo, lo, c_dl)
    store(lo, lo)
    arrived(up & right, lo, hi, c_dr)
    store(lo, hi)
    arrived(down & left, hi, lo, c_ul)
    store(hi, lo)
    arrived(down & right, hi, hi, c_ur)
    store(hi, hi)
    arrived(left, spans[2], lo, to_r[2])
    store(mid, lo)
    arrived(right, spans[2], hi, to_l[2])
    store(mid, hi)
    for one in stored:
        one.wait()

    for there, some in (
        (left, to_l),
        (right, to_r),
        (up, [to_u]),
        (down, [to_d]),
        (up & left, [c_ul]),
        (up & right, [c_ur]),
        (down & left, [c_dl]),
        (down & right, [c_dr]),
    ):

        @pl.when(there)
        def _(some=some):
            for one in some:
                one.wait_send()


def halo(tile):
    return pl.pallas_call(
        halo_kernel,
        out_shape=jax.ShapeDtypeStruct((2, E, E), jnp.float32),
        in_specs=[pl.BlockSpec(memory_space=pl.ANY)],
        out_specs=pl.BlockSpec(memory_space=pl.ANY),
        scratch_shapes=[
            pltpu.VMEM((2, E, E), jnp.float32),
            pltpu.SemaphoreType.DMA((12,)),
            pltpu.SemaphoreType.DMA((12,)),
            pltpu.SemaphoreType.DMA,
            pltpu.SemaphoreType.DMA((9,)),
        ],
        compiler_params=pltpu.CompilerParams(collective_id=0, has_side_effects=True, vmem_limit_bytes=32 << 20),
    )(tile)


STEP = 32


def dot(a, b):
    return jnp.dot(a, b, preferred_element_type=jnp.float32)


def slots_kernel(
    corners, live, padded, probe, photons, fwd, bwd, grad, pacc, window, counts, patch, terms, rows_in, cols_in, wave, win_sem, cnt_sem
):
    def box(slot):
        top, left = corners[slot, 0] + RIM, corners[slot, 1] + RIM
        top0 = pl.multiple_of(jnp.minimum(top // 8 * 8, E - WROWS), 8)
        left0 = pl.multiple_of(jnp.minimum(left // 128 * 128, E - WCOLS), 128)
        return top0, left0, top - top0, left - left0

    def fetches(slot):
        top0, left0, _, _ = box(slot)
        return (
            pltpu.make_async_copy(
                padded.at[:, pl.ds(top0, WROWS), pl.ds(left0, WCOLS)], window.at[slot], win_sem.at[slot]
            ),
            pltpu.make_async_copy(photons.at[slot], counts.at[slot], cnt_sem.at[slot]),
        )

    for slot in range(SLOTS):
        for one in fetches(slot):
            one.start()
    grad[...] = jnp.zeros_like(grad)
    pacc[...] = jnp.zeros_like(pacc)
    lane = lax.broadcasted_iota(jnp.int32, (8, 128), 1)
    sublane = lax.broadcasted_iota(jnp.int32, (8, 128), 0)
    nothing = jnp.zeros((8, 128), jnp.float32)

    def visit(slot, carry):
        top0, left0, down, over = box(slot)
        for one in fetches(slot):
            one.wait()
        back_by, ahead_by = lax.rem(128 - over, 128), lax.rem(over, 128)
        up_by, down_by = lax.rem(8 - down, 8), lax.rem(down, 8)
        for k in range(2):
            before = None
            for i in range(WROWS // 8):
                a, b, d = (
                    pltpu.roll(window[slot, k, 8 * i : 8 * i + 8, 128 * j : 128 * j + 128], back_by, 1) for j in range(3)
                )
                keep = lane < 128 - over
                now = tuple(pltpu.roll(v, up_by, 0) for v in (jnp.where(keep, a, b), jnp.where(keep, b, d)))
                if i:
                    for j in range(2):
                        patch[k, 8 * i - 8 : 8 * i, 128 * j : 128 * j + 128] = jnp.where(
                            sublane < 8 - down, before[j], now[j]
                        )
                before = now
        for m in range(M):
            for r in range(0, S, STEP):
                here = pl.ds(r, STEP)
                o_re, o_im = patch[0, here, :], patch[1, here, :]
                p_re, p_im = probe[m, 0, here, :], probe[m, 1, here, :]
                rows_in[m, r : r + STEP, :] = (p_re * o_re - p_im * o_im).astype(jnp.bfloat16)
                rows_in[m, S + r : S + r + STEP, :] = (p_re * o_im + p_im * o_re).astype(jnp.bfloat16)
            half = dot(fwd[...], rows_in[m])
            cols_in[m, :, 0:S] = half[0:S].astype(jnp.bfloat16)
            cols_in[m, :, S:] = half[S:].astype(jnp.bfloat16)
            wave[m] = dot(cols_in[m], bwd[...])
        for r in range(0, S, STEP):
            here = pl.ds(r, STEP)
            total = None
            for m in range(M):
                w_re, w_im = wave[m, here, 0:S], wave[m, here, S:]
                term = w_re * w_re + w_im * w_im
                total = term if m == 0 else total + term
            factor = 1.0 - counts[slot, here, :].astype(jnp.float32) / (total + background)
            for m in range(M):
                rows_in[m, r : r + STEP, :] = (factor * wave[m, here, 0:S]).astype(jnp.bfloat16)
                rows_in[m, S + r : S + r + STEP, :] = (factor * wave[m, here, S:]).astype(jnp.bfloat16)
        for m in range(M):
            back = dot(bwd[...], rows_in[m])
            cols_in[m, :, 0:S] = back[0:S].astype(jnp.bfloat16)
            cols_in[m, :, S:] = back[S:].astype(jnp.bfloat16)
            wave[m] = dot(cols_in[m], fwd[...])
        for r in range(0, S, STEP):
            here = pl.ds(r, STEP)
            o_re, o_im = patch[0, here, :], patch[1, here, :]
            t_re = t_im = None
            for m in range(M):
                c_re, c_im = wave[m, here, 0:S], wave[m, here, S:]
                p_re, p_im = probe[m, 0, here, :], probe[m, 1, here, :]
                a_re, a_im = p_re * c_re + p_im * c_im, p_re * c_im - p_im * c_re
                t_re, t_im = (a_re, a_im) if m == 0 else (t_re + a_re, t_im + a_im)
                pacc[m, 0, here, :] += o_re * c_re + o_im * c_im
                pacc[m, 1, here, :] += o_re * c_im - o_im * c_re
            terms[0, here, :], terms[1, here, :] = t_re, t_im
        inside = lane >= over
        for k in range(2):
            before = (nothing, nothing)
            for i in range(WROWS // 8):
                now = (nothing, nothing)
                if i < S // 8:
                    now = tuple(
                        pltpu.roll(terms[k, 8 * i : 8 * i + 8, 128 * j : 128 * j + 128], down_by, 0) for j in range(2)
                    )
                a, b = (pltpu.roll(jnp.where(sublane >= down, now[j], before[j]), ahead_by, 1) for j in range(2))
                before = now
                spread = (jnp.where(inside, a, 0.0), jnp.where(inside, b, a), jnp.where(inside, 0.0, b))
                rows = pl.ds(pl.multiple_of(top0 + 8 * i, 8), 8)
                for j in range(3):
                    grad[k, rows, pl.ds(pl.multiple_of(left0 + j * 128, 128), 128)] += spread[j]
        return carry

    lax.fori_loop(0, live[0, 0], visit, 0)

    def drain(slot, carry):
        for one in fetches(slot):
            one.wait()
        return carry

    lax.fori_loop(live[0, 0], SLOTS, drain, 0)


def slots(padded, probe, photons, corners, live):
    fwd = dft_table(S)
    vmem, smem, anywhere = (pl.BlockSpec(memory_space=m) for m in (pltpu.VMEM, pltpu.SMEM, pl.ANY))
    return pl.pallas_call(
        slots_kernel,
        out_shape=(
            jax.ShapeDtypeStruct((2, E, E), jnp.float32),
            jax.ShapeDtypeStruct((M, 2, S, S), jnp.float32),
        ),
        in_specs=[smem, smem, anywhere, vmem, anywhere, vmem, vmem],
        out_specs=(vmem, vmem),
        scratch_shapes=[
            pltpu.VMEM((SLOTS, 2, WROWS, WCOLS), jnp.float32),
            pltpu.VMEM((SLOTS, S, S), jnp.int32),
            pltpu.VMEM((2, S, S), jnp.float32),
            pltpu.VMEM((2, S, S), jnp.float32),
            pltpu.VMEM((M, 2 * S, S), jnp.bfloat16),
            pltpu.VMEM((M, S, 2 * S), jnp.bfloat16),
            pltpu.VMEM((M, S, 2 * S), jnp.float32),
            pltpu.SemaphoreType.DMA((SLOTS,)),
            pltpu.SemaphoreType.DMA((SLOTS,)),
        ],
        compiler_params=pltpu.CompilerParams(vmem_limit_bytes=48 << 20),
    )(corners, live, padded, probe, photons, fwd, fwd.T)


GROUPS = M * 2 * S // 8
HALF = GROUPS // 2
PARTS = ((0, 64, ("x", "z", "y")), (64, 32, ("y", "z", "x")), (96, 32, ("z", "x", "y")))
AXES = {"x": 4, "y": 4, "z": 8}


def sums_kernel(grad, pacc, core_out, probe_out, above, below, left_in, right_in, acc, from_twin, *rest):
    n_parts = len(PARTS)
    ins = [rest[3 * i : 3 * i + 3] for i in range(n_parts)]
    sums = [rest[3 * n_parts + 2 * i : 3 * n_parts + 2 * i + 2] for i in range(n_parts)]
    send_sem, recv_sem = rest[5 * n_parts :]
    r, c = lax.axis_index("rows"), lax.axis_index("cols")
    n_r, n_c = lax.axis_size("rows"), lax.axis_size("cols")
    up, down, left, right = r > 0, r < n_r - 1, c > 0, c < n_c - 1
    to_up, to_down, to_left, to_right = (r - 1, c), (r + 1, c), (r, c - 1), (r, c + 1)
    core = r % 2
    at = {"x": r // 16 * 2 + c // 4, "y": c % 4, "z": r // 2 % 8}
    twin = (r + 1 - 2 * core, c)

    def peer(axis, k):
        place = dict(at)
        place[axis] = (at[axis] + k) % AXES[axis]
        return (place["x"] // 2 * 16 + place["z"] * 2 + core, place["x"] % 2 * 4 + place["y"])

    sides = ((up, to_up), (down, to_down), (left, to_left), (right, to_right))
    peers = [twin] + [peer(axis, k) for axis in AXES for k in range(1, AXES[axis])]
    barrier = pltpu.get_barrier_semaphore()
    for device in peers:
        pl.semaphore_signal(barrier, inc=1, device_id=device, device_id_type=MESH)
    for there, device in sides:

        @pl.when(there)
        def _(device=device):
            pl.semaphore_signal(barrier, inc=1, device_id=device, device_id_type=MESH)

    pl.semaphore_wait(barrier, len(peers) + sum(jnp.where(there, 1, 0) for there, _ in sides))

    count = [0]

    def copy(src, dst, device):
        index = count[0]
        count[0] += 1
        return pltpu.make_async_remote_copy(
            src_ref=src,
            dst_ref=dst,
            send_sem=send_sem.at[index],
            recv_sem=recv_sem.at[index],
            device_id=device,
            device_id_type=MESH,
        )

    sent = []

    def go(some):
        for one in some:
            one.start()
        sent.extend(some)
        return some

    first = HALF * core
    other = HALF * (1 - core)
    stage0 = [
        go([copy(pacc.at[pl.ds(other + p0, size)], from_twin.at[pl.ds(p0, size)], twin)])[0] for p0, size, _ in PARTS
    ]
    lo, hi = pl.ds(0, RIM), pl.ds(RIM + T, RIM)
    bands = (pl.ds(0, RIM), pl.ds(RIM + T, RIM), pl.ds(RIM, T))
    to_u = [copy(grad.at[:, lo, b], below.at[:, :, b], to_up) for b in bands]
    to_d = [copy(grad.at[:, hi, b], above.at[:, :, b], to_down) for b in bands]
    spans = ((2 * RIM, T - 2 * RIM), (RIM, RIM), (T, RIM))
    to_l = [copy(grad.at[:, pl.ds(s, n), lo], right_in.at[:, pl.ds(s - RIM, n), :], to_left) for s, n in spans]
    to_r = [copy(grad.at[:, pl.ds(s, n), hi], left_in.at[:, pl.ds(s - RIM, n), :], to_right) for s, n in spans]

    def when_start(there, some):
        @pl.when(there)
        def _():
            for one in some:
                one.start()

    when_start(up, to_u)
    when_start(down, to_d)
    when_start(left, to_l[:1])
    when_start(right, to_r[:1])

    stage1 = []
    for i, (p0, size, axes) in enumerate(PARTS):
        stage0[i].wait_recv()
        acc[pl.ds(p0, size)] = pacc[pl.ds(first + p0, size)] + from_twin[pl.ds(p0, size)]
        n = AXES[axes[0]]
        s = size // n
        some = []
        for k in range(1, n):
            to = (at[axes[0]] + k) % n
            some.append(copy(acc.at[pl.ds(p0 + s * to, s)], ins[i][0].at[k - 1], peer(axes[0], k)))
        stage1.append(go(some))

    @pl.when(up)
    def _():
        for one in to_d[:2]:
            one.wait_recv()
        grad[:, RIM : 2 * RIM, 0:RIM] += above[:, :, 0:RIM]
        grad[:, RIM : 2 * RIM, RIM + T :] += above[:, :, RIM + T :]

    when_start(left, to_l[1:2])
    when_start(right, to_r[1:2])

    @pl.when(down)
    def _():
        for one in to_u[:2]:
            one.wait_recv()
        grad[:, T : T + RIM, 0:RIM] += below[:, :, 0:RIM]
        grad[:, T : T + RIM, RIM + T :] += below[:, :, RIM + T :]

    when_start(left, to_l[2:])
    when_start(right, to_r[2:])

    stage2 = []
    for i, (p0, size, axes) in enumerate(PARTS):
        n = AXES[axes[0]]
        s = size // n
        for one in stage1[i]:
            one.wait_recv()
        total = acc[pl.ds(p0 + s * at[axes[0]], s)]
        for k in range(n - 1):
            total = total + ins[i][0][k]
        sums[i][0][...] = total
        n2 = AXES[axes[1]]
        s2 = s // n2
        some = []
        for k in range(1, n2):
            to = (at[axes[1]] + k) % n2
            some.append(copy(sums[i][0].at[pl.ds(s2 * to, s2)], ins[i][1].at[k - 1], peer(axes[1], k)))
        stage2.append(go(some))

    stage3 = []
    for i, (p0, size, axes) in enumerate(PARTS):
        n2 = AXES[axes[1]]
        s2 = size // AXES[axes[0]] // n2
        for one in stage2[i]:
            one.wait_recv()
        total = sums[i][0][pl.ds(s2 * at[axes[1]], s2)]
        for k in range(n2 - 1):
            total = total + ins[i][1][k]
        mine = ins[i][2].at[at[axes[2]]]
        sums[i][1][...] = total
        ins[i][2][at[axes[2]]] = total
        stage3.append(go([copy(sums[i][1], mine, peer(axes[2], k)) for k in range(1, AXES[axes[2]])]))

    scale = 1.0 / math.sqrt(n_r * n_c)
    gather2 = []
    for i, (p0, size, axes) in enumerate(PARTS):
        s = size // AXES[axes[0]]
        s2 = s // AXES[axes[1]]
        for one in stage3[i]:
            one.wait_recv()
        total = ins[i][2][0]
        for j in range(1, AXES[axes[2]]):
            total = total + ins[i][2][j]
        place = pl.ds(first + p0 + s * at[axes[0]] + s2 * at[axes[1]], s2)
        probe_out[place] = total * scale
        block = probe_out.at[place]
        gather2.append(go([copy(block, block, peer(axes[1], k)) for k in range(1, AXES[axes[1]])]))
    gather1 = []
    for i, (p0, size, axes) in enumerate(PARTS):
        s = size // AXES[axes[0]]
        for one in gather2[i]:
            one.wait_recv()
        block = probe_out.at[pl.ds(first + p0 + s * at[axes[0]], s)]
        gather1.append(go([copy(block, block, peer(axes[0], k)) for k in range(1, AXES[axes[0]])]))
    gather0 = []
    for i, (p0, size, axes) in enumerate(PARTS):
        for one in gather1[i]:
            one.wait_recv()
        block = probe_out.at[pl.ds(first + p0, size)]
        gather0.append(go([copy(block, block, twin)])[0])

    core_out[...] = grad[:, RIM : RIM + T, RIM : RIM + T]

    @pl.when(up)
    def _():
        to_d[2].wait_recv()
        core_out[:, 0:RIM, :] += above[:, :, RIM : RIM + T]

    @pl.when(down)
    def _():
        to_u[2].wait_recv()
        core_out[:, T - RIM :, :] += below[:, :, RIM : RIM + T]

    @pl.when(left)
    def _():
        for one in to_r:
            one.wait_recv()
        core_out[:, :, 0:RIM] += left_in[...]

    @pl.when(right)
    def _():
        for one in to_l:
            one.wait_recv()
        core_out[:, :, T - RIM :] += right_in[...]

    for there, some in ((up, to_u), (down, to_d), (left, to_l), (right, to_r)):

        @pl.when(there)
        def _(some=some):
            for one in some:
                one.wait_send()

    for one in gather0:
        one.wait_recv()
    for one in sent:
        one.wait_send()


def sums(grad, pacc):
    ins, parts = [], []
    copies = 2 * len(PARTS) + 12
    for _p0, size, axes in PARTS:
        n = [AXES[a] for a in axes]
        s = size // n[0]
        s2 = s // n[1]
        ins += [
            pltpu.VMEM((n[0] - 1, s, 8, S), jnp.float32),
            pltpu.VMEM((n[1] - 1, s2, 8, S), jnp.float32),
            pltpu.VMEM((n[2], s2, 8, S), jnp.float32),
        ]
        parts += [pltpu.VMEM((s, 8, S), jnp.float32), pltpu.VMEM((s2, 8, S), jnp.float32)]
        copies += 2 * (n[0] + n[1] - 2) + n[2] - 1
    vmem = pl.BlockSpec(memory_space=pltpu.VMEM)
    core, probe_grad = pl.pallas_call(
        sums_kernel,
        out_shape=(
            jax.ShapeDtypeStruct((2, T, T), jnp.float32),
            jax.ShapeDtypeStruct((GROUPS, 8, S), jnp.float32),
        ),
        in_specs=[vmem, vmem],
        out_specs=(vmem, vmem),
        scratch_shapes=[
            pltpu.VMEM((2, RIM, E), jnp.float32),
            pltpu.VMEM((2, RIM, E), jnp.float32),
            pltpu.VMEM((2, T, RIM), jnp.float32),
            pltpu.VMEM((2, T, RIM), jnp.float32),
            pltpu.VMEM((HALF, 8, S), jnp.float32),
            pltpu.VMEM((HALF, 8, S), jnp.float32),
            *ins,
            *parts,
            pltpu.SemaphoreType.DMA((copies,)),
            pltpu.SemaphoreType.DMA((copies,)),
        ],
        compiler_params=pltpu.CompilerParams(collective_id=1, has_side_effects=True, vmem_limit_bytes=48 << 20),
    )(grad, pacc.reshape(GROUPS, 8, S))
    return core, probe_grad.reshape(M, 2, S, S)


def on_device(object_field, probe, photons, positions, live_counts):
    padded = halo(object_field)
    grad, pacc = slots(padded, probe, photons[0, 0], positions[0, 0], live_counts)
    return sums(grad, pacc)


def solution(mesh):
    in_specs = (
        P(None, "rows", "cols"),
        P(),
        P("rows", "cols", None, None, None),
        P("rows", "cols", None, None),
        P("rows", "cols"),
    )
    out_specs = (P(None, "rows", "cols"), P())
    return jax.shard_map(on_device, mesh=mesh, in_specs=in_specs, out_specs=out_specs, check_vma=False)
```

```python
import math

import jax
import jax.numpy as jnp
import numpy as np
from jax import lax
from jax.experimental import pallas as pl
from jax.experimental.pallas import tpu as pltpu
from jax.sharding import PartitionSpec as P

MESH = pl.DeviceIdType.MESH
background = 1.0
S = 256
RIM = 128
T = 512
E = T + 2 * RIM
M = 4
SLOTS = 4
WROWS, WCOLS = S // 8 + 1, S // 128 + 1
ROWS, COLS = E // 8 + 1, E // 128 + 1
STEP = 32
GROUPS = M * 2 * S // 8
PER_MODE = GROUPS // M
PART = PER_MODE // 2
AXES = {"x": 4, "y": 4, "z": 8}
ORDERS = (("y", "x", "z"), ("x", "y", "z"), ("y", "x", "z"), ("x", "y", "z"))
N_SUM = sum(2 + 2 * (AXES[a] - 1) + 2 * (AXES[b] - 1) + AXES[d] - 1 for a, b, d in ORDERS)
N_COPIES = 24 + 48 + N_SUM


def dft_table(wave_size):
    ramp = np.arange(wave_size, dtype=np.int32)
    phases = ramp[:, None] * ramp[None, :] % wave_size
    angles = phases.astype(np.float32) * np.float32(2.0 * math.pi / wave_size)
    scaling = np.float32(1.0 / math.sqrt(wave_size))
    cos_t = (np.cos(angles) * scaling).astype(jnp.bfloat16)
    sin_t = (np.sin(angles) * scaling).astype(jnp.bfloat16)
    return np.block([[cos_t, sin_t], [-sin_t, cos_t]])


def dot(a, b):
    return jnp.dot(a, b, preferred_element_type=jnp.float32)


def box(corners, slot):
    top, left = corners[0, slot] + RIM, corners[1, slot] + RIM
    shift = lax.shift_right_logical
    return shift(top, 3), shift(left, 7), lax.bitwise_and(top, 7), lax.bitwise_and(left, 127)


def forward(slot, corners, live, padded, probe, counts, fwd, bwd, patch, rows_in, cols_in, wave):
    lane = lax.broadcasted_iota(jnp.int32, (8, 128), 1)
    sublane = lax.broadcasted_iota(jnp.int32, (8, 128), 0)
    top0, left0, down, over = box(corners, slot)
    back_by, up_by = lax.bitwise_and(128 - over, 127), lax.bitwise_and(8 - down, 7)
    keep = lane < 128 - over
    for k in range(2):
        before = None
        for i in range(WROWS):
            a, b, d = (pltpu.roll(padded[k, top0 + i, left0 + j], back_by, 1) for j in range(3))
            now = tuple(pltpu.roll(v, up_by, 0) for v in (jnp.where(keep, a, b), jnp.where(keep, b, d)))
            if i:
                for j in range(2):
                    patch[slot, k, 8 * i - 8 : 8 * i, 128 * j : 128 * j + 128] = jnp.where(
                        sublane < 8 - down, before[j], now[j]
                    )
            before = now
    for m in range(M):
        for r in range(0, S, STEP):
            here = pl.ds(r, STEP)
            o_re, o_im = patch[slot, 0, here, :], patch[slot, 1, here, :]
            p_re, p_im = probe[m, 0, here, :], probe[m, 1, here, :]
            rows_in[slot, m, r : r + STEP, :] = (p_re * o_re - p_im * o_im).astype(jnp.bfloat16)
            rows_in[slot, m, S + r : S + r + STEP, :] = (p_re * o_im + p_im * o_re).astype(jnp.bfloat16)
        half = dot(fwd[...], rows_in[slot, m])
        cols_in[m, :, 0:S] = half[0:S].astype(jnp.bfloat16)
        cols_in[m, :, S:] = half[S:].astype(jnp.bfloat16)
        wave[m] = dot(cols_in[m], bwd[...])
    alive = jnp.full((STEP, S), live[0, 0]) > slot
    for r in range(0, S, STEP):
        here = pl.ds(r, STEP)
        total = None
        for m in range(M):
            w_re, w_im = wave[m, here, 0:S], wave[m, here, S:]
            term = w_re * w_re + w_im * w_im
            total = term if m == 0 else total + term
        factor = 1.0 - counts[slot, here, :].astype(jnp.float32) / (total + background)
        factor = jnp.where(alive, factor, 0.0)
        for m in range(M):
            rows_in[slot, m, r : r + STEP, :] = (factor * wave[m, here, 0:S]).astype(jnp.bfloat16)
            rows_in[slot, m, S + r : S + r + STEP, :] = (factor * wave[m, here, S:]).astype(jnp.bfloat16)


def backward(m, probe, fwd, bwd, patch, rows_in, cols_in, wave, terms, pacc):
    for slot in range(SLOTS):
        back = dot(bwd[...], rows_in[slot, m])
        cols_in[slot, :, 0:S] = back[0:S].astype(jnp.bfloat16)
        cols_in[slot, :, S:] = back[S:].astype(jnp.bfloat16)
        wave[slot] = dot(cols_in[slot], fwd[...])
    for r in range(0, S, STEP):
        here = pl.ds(r, STEP)
        p_re, p_im = probe[m, 0, here, :], probe[m, 1, here, :]
        q_re = q_im = None
        for slot in range(SLOTS):
            c_re, c_im = wave[slot, here, 0:S], wave[slot, here, S:]
            o_re, o_im = patch[slot, 0, here, :], patch[slot, 1, here, :]
            a_re, a_im = p_re * c_re + p_im * c_im, p_re * c_im - p_im * c_re
            if m:
                a_re, a_im = terms[slot, 0, here, :] + a_re, terms[slot, 1, here, :] + a_im
            terms[slot, 0, here, :], terms[slot, 1, here, :] = a_re, a_im
            b_re, b_im = o_re * c_re + o_im * c_im, o_re * c_im - o_im * c_re
            q_re, q_im = (b_re, b_im) if slot == 0 else (q_re + b_re, q_im + b_im)
        for i in range(STEP // 8):
            g = m * PER_MODE + r // 8 + i
            pacc[g] = q_re[8 * i : 8 * i + 8]
            pacc[g + PART] = q_im[8 * i : 8 * i + 8]


def place(slot, corners, terms, spread):
    lane = lax.broadcasted_iota(jnp.int32, (8, 128), 1)
    sublane = lax.broadcasted_iota(jnp.int32, (8, 128), 0)
    nothing = jnp.zeros((8, 128), jnp.float32)
    _, _, down, over = box(corners, slot)
    ahead_by, down_by = lax.bitwise_and(over, 127), lax.bitwise_and(down, 7)
    inside = lane >= over
    for k in range(2):
        before = (nothing, nothing)
        for i in range(WROWS):
            now = (nothing, nothing)
            if i < S // 8:
                now = tuple(
                    pltpu.roll(terms[slot, k, 8 * i : 8 * i + 8, 128 * j : 128 * j + 128], down_by, 0) for j in range(2)
                )
            a, b = (pltpu.roll(jnp.where(sublane >= down, now[j], before[j]), ahead_by, 1) for j in range(2))
            before = now
            for j, v in enumerate((jnp.where(inside, a, 0.0), jnp.where(inside, b, a), jnp.where(inside, 0.0, b))):
                spread[slot, k, i + 1, j + 1] = v


def gather(corners, spread, row0, rows, cols, store):
    places = [box(corners, slot)[:2] for slot in range(SLOTS)]
    at_col = [[lax.max(lax.min(c - left0, WCOLS), -1) + 1 for c in cols] for _, left0 in places]

    def body(i, carry):
        at_row = [lax.max(lax.min(row0 // 8 + i - top0, WROWS), -1) + 1 for top0, _ in places]
        for j in range(len(cols)):
            for k in range(2):
                value = None
                for slot in range(SLOTS):
                    one = spread[slot, k, at_row[slot], at_col[slot][j]]
                    value = one if slot == 0 else value + one
                store(k, pl.multiple_of(8 * i, 8), j, value)
        return carry

    lax.fori_loop(0, rows // 8, body, 0, unroll=2)


def kernel(
    corners, live, tile, probe_hbm, photons, fwd_hbm, bwd_hbm, core_out, probe_out,
    padded, probe, counts, fwd, bwd, patch, rows_in, cols_in, wave, terms, spread, pacc,
    g_up, g_down, g_left, g_right, above, below, left_in, right_in, from_twin, acc,
    in1, in2, in3, sum1, sum2, passing, passing2, core_sum, probe_sum, send_sem, recv_sem, load_sem,
):
    r, c = lax.axis_index("rows"), lax.axis_index("cols")
    n_r, n_c = lax.axis_size("rows"), lax.axis_size("cols")
    up, down, left, right = r > 0, r < n_r - 1, c > 0, c < n_c - 1
    to_up, to_down, to_left, to_right = (r - 1, c), (r + 1, c), (r, c - 1), (r, c + 1)
    sides = ((up, to_up), (down, to_down), (left, to_left), (right, to_right))
    core = r % 2
    at = {"x": r // 16 * 2 + c // 4, "y": c % 4, "z": r // 2 % 8}
    twin = (r + 1 - 2 * core, c)

    def peer(axis, k):
        spot = dict(at)
        spot[axis] = (at[axis] + k) % AXES[axis]
        return (spot["x"] // 2 * 16 + spot["z"] * 2 + core, spot["x"] % 2 * 4 + spot["y"])

    lo, mid, hi = pl.ds(0, RIM), pl.ds(RIM, T), pl.ds(RIM + T, RIM)
    r_lo, r_mid, r_hi = pl.ds(0, RIM // 8), pl.ds(RIM // 8, T // 8), pl.ds((RIM + T) // 8, RIM // 8)
    c_lo, c_mid, c_hi = pl.ds(0, 1), pl.ds(1, T // 128), pl.ds(1 + T // 128, 1)
    loads = [
        pltpu.make_async_copy(src, dst, load_sem.at[i])
        for i, (src, dst) in enumerate(
            ((tile, padded.at[:, r_mid, c_mid]), (probe_hbm, probe), (fwd_hbm, fwd), (bwd_hbm, bwd), (photons, counts))
        )
    ]
    loads[0].start()
    n_half, middle = n_r // 2, (c == n_c // 2 - 1) | (c == n_c // 2)
    at_corner, past = (c == 0) | (c == n_c - 1), jnp.where(c < n_c // 2, n_c - 1, 0)
    back = jnp.where(c == 0, n_c // 2, n_c // 2 - 1)
    way_down = ((r == n_half - 1) & middle, (n_r - 1, past), (r == n_r - 1) & at_corner, (n_half - 1, back), (n_half, back), (r == n_half) & middle)
    way_up = ((r == n_half) & middle, (0, past), (r == 0) & at_corner, (n_half, back), (n_half - 1, back), (r == n_half - 1) & middle)
    ways = (way_down, way_up)
    peers = [twin] + [peer(axis, k) for axis in AXES for k in range(1, AXES[axis])]
    barrier = pltpu.get_barrier_semaphore()
    for there, device in sides:

        @pl.when(there)
        def _(device=device):
            pl.semaphore_signal(barrier, inc=1, device_id=device, device_id_type=MESH)

    for source, relay, is_relay, from_device, _, target in ways:

        @pl.when(is_relay)
        def _(device=from_device):
            pl.semaphore_signal(barrier, inc=1, device_id=device, device_id_type=MESH)

        @pl.when(target)
        def _(device=relay):
            pl.semaphore_signal(barrier, inc=1, device_id=device, device_id_type=MESH)

    for device in peers:
        pl.semaphore_signal(barrier, inc=1, device_id=device, device_id_type=MESH)
    for one in loads[1:]:
        one.start()
    loads[0].wait()
    pl.semaphore_wait(barrier, len(peers) + sum(jnp.where(there, 1, 0) for there, _ in sides) + sum(jnp.where(way[0], 1, 0) + jnp.where(way[2], 1, 0) for way in ways))

    count = [0]

    def copy(src, dst, device):
        index = count[0]
        count[0] += 1
        return pltpu.make_async_remote_copy(
            src_ref=src,
            dst_ref=dst,
            send_sem=send_sem.at[index],
            recv_sem=recv_sem.at[index],
            device_id=device,
            device_id_type=MESH,
        )

    sent = []

    def go(some, there=None):
        if there is None:
            for one in some:
                one.start()
        else:

            @pl.when(there)
            def _():
                for one in some:
                    one.start()

        sent.append((there, some))
        return some

    def relayed(way, pieces):
        legs = [(copy(src, buf, way[1]), copy(buf, dst, way[4])) for src, buf, dst in pieces]

        def depart(*some):
            go([legs[i][0] for i in some], way[0])

        def pass_on(*some):
            for i in some:

                @pl.when(way[2])
                def _(i=i):
                    legs[i][0].wait_recv()

                go([legs[i][1]], way[2])

        def arrive(*some):
            for i in some:
                legs[i][1].wait_recv()

        return depart, pass_on, arrive

    down_direct, up_direct = down & jnp.logical_not(way_down[0]), up & jnp.logical_not(way_up[0])
    above_direct, below_direct = up & jnp.logical_not(way_down[5]), down & jnp.logical_not(way_up[5])

    r_near, r_far = pl.ds(RIM // 8, RIM // 8), pl.ds(T // 8, RIM // 8)
    c_near, c_far = pl.ds(1, 1), pl.ds(T // 128, 1)
    spans = (r_near, r_far, pl.ds(2 * RIM // 8, (T - 2 * RIM) // 8))
    to_l = [copy(padded.at[:, s, c_near], padded.at[:, s, c_hi], to_left) for s in spans]
    to_r = [copy(padded.at[:, s, c_far], padded.at[:, s, c_lo], to_right) for s in spans]
    to_u = copy(padded.at[:, r_near, c_mid], padded.at[:, r_hi, c_mid], to_up)
    to_d = copy(padded.at[:, r_far, c_mid], padded.at[:, r_lo, c_mid], to_down)
    c_ul = copy(padded.at[:, r_near, c_lo], padded.at[:, r_hi, c_lo], to_up)
    c_ur = copy(padded.at[:, r_near, c_hi], padded.at[:, r_hi, c_hi], to_up)
    c_dl = copy(padded.at[:, r_far, c_lo], padded.at[:, r_lo, c_lo], to_down)
    c_dr = copy(padded.at[:, r_far, c_hi], padded.at[:, r_lo, c_hi], to_down)
    blocks = [pl.ds(1 + i, 1) for i in range(T // 128)] + [c_lo, c_hi]
    strips_in = range(T // 128)
    relay_down = relayed(way_down, [(padded.at[:, r_far, b], passing.at[:, :, b], padded.at[:, r_lo, b]) for b in blocks])
    relay_up = relayed(way_up, [(padded.at[:, r_near, b], passing.at[:, :, b], padded.at[:, r_hi, b]) for b in blocks])
    for i in range(3):
        go([to_l[i]], left)
        go([to_r[i]], right)
        if i == 0:
            go([to_u], up_direct)
            go([to_d], down_direct)
            relay_down[0](*strips_in)
            relay_up[0](*strips_in)

    for slot in range(SLOTS):
        spread[slot, :, 0] = jnp.zeros((2, WCOLS + 2, 8, 128), jnp.float32)
        spread[slot, :, WROWS + 1] = jnp.zeros((2, WCOLS + 2, 8, 128), jnp.float32)
        spread[slot, :, :, 0] = jnp.zeros((2, WROWS + 2, 8, 128), jnp.float32)
        spread[slot, :, :, WCOLS + 1] = jnp.zeros((2, WROWS + 2, 8, 128), jnp.float32)
    padded[:, ROWS - 1] = jnp.zeros((2, COLS, 8, 128), jnp.float32)
    padded[:, :, COLS - 1] = jnp.zeros((2, ROWS, 8, 128), jnp.float32)

    def zeroed(there, rows, cols):
        @pl.when(jnp.logical_not(there))
        def _():
            padded[:, rows, cols] = jnp.zeros((2, rows.size, cols.size, 8, 128), jnp.float32)

    def arrived(there, one, way=None, relay=None, some=()):
        @pl.when(there)
        def _():
            one.wait_recv()

        if way is not None:

            @pl.when(way[5])
            def _():
                relay[2](*some)

    for there, rows, cols in (
        (left, r_mid, c_lo), (right, r_mid, c_hi), (up, r_lo, c_mid), (down, r_hi, c_mid),
        (up & left, r_lo, c_lo), (up & right, r_lo, c_hi), (down & left, r_hi, c_lo), (down & right, r_hi, c_hi),
    ):
        zeroed(there, rows, cols)
    corner_l, corner_r = len(blocks) - 2, len(blocks) - 1
    relay_down[1](0)
    relay_up[1](0)
    arrived(left, to_r[0])
    go([c_ul], left & up_direct)
    relay_up[0](corner_l)
    arrived(right, to_l[0])
    go([c_ur], right & up_direct)
    relay_up[0](corner_r)
    relay_down[1](1)
    relay_up[1](1)
    arrived(left, to_r[1])
    go([c_dl], left & down_direct)
    relay_down[0](corner_l)
    arrived(right, to_l[1])
    go([c_dr], right & down_direct)
    relay_down[0](corner_r)
    for i in (2, 3, corner_l, corner_r):
        relay_down[1](i)
        relay_up[1](i)
    arrived(above_direct, to_d, way_down, relay_down, strips_in)
    arrived(below_direct, to_u, way_up, relay_up, strips_in)
    arrived(left, to_r[2])
    arrived(right, to_l[2])
    arrived(above_direct & left, c_dl, way_down, relay_down, (corner_l,))
    arrived(above_direct & right, c_dr, way_down, relay_down, (corner_r,))
    arrived(below_direct & left, c_ul, way_up, relay_up, (corner_l,))
    arrived(below_direct & right, c_ur, way_up, relay_up, (corner_r,))
    for one in loads[1:]:
        one.wait()

    def visit(slot, carry):
        forward(slot, corners, live, padded, probe, counts, fwd, bwd, patch, rows_in, cols_in, wave)
        return carry

    lax.fori_loop(0, SLOTS, visit, 0)

    first, other = PART * core, PART * (1 - core)
    scale = 1.0 / math.sqrt(n_r * n_c)
    flying = {}

    def sizes(m):
        a, b, d = ORDERS[m]
        return a, b, d, PART // AXES[a], PART // AXES[a] // AXES[b]

    def swap(m):
        src = pacc.at[pl.ds(m * PER_MODE + other, PART)]
        flying[m] = go([copy(src, from_twin.at[pl.ds(m * PART, PART)], twin)])

    def landed(m):
        for one in flying[m]:
            one.wait_recv()

    def reduce1(m):
        a, _, _, s, _ = sizes(m)
        landed(m)
        here = pl.ds(m * PART, PART)
        acc[here] = pacc[pl.ds(m * PER_MODE + first, PART)] + from_twin[here]
        flying[m] = go(
            [
                copy(
                    acc.at[pl.ds(m * PART + s * ((at[a] + k) % AXES[a]), s)],
                    in1.at[m, pl.ds((k - 1) * s, s)],
                    peer(a, k),
                )
                for k in range(1, AXES[a])
            ]
        )

    def reduce2(m):
        a, b, _, s, s2 = sizes(m)
        landed(m)
        total = acc[pl.ds(m * PART + s * at[a], s)]
        for k in range(AXES[a] - 1):
            total = total + in1[m, k * s : (k + 1) * s]
        sum1[m, 0:s] = total
        flying[m] = go(
            [
                copy(
                    sum1.at[m, pl.ds(s2 * ((at[b] + k) % AXES[b]), s2)],
                    in2.at[m, pl.ds((k - 1) * s2, s2)],
                    peer(b, k),
                )
                for k in range(1, AXES[b])
            ]
        )

    def reduce3(m):
        _, b, d, _, s2 = sizes(m)
        landed(m)
        total = sum1[m, pl.ds(s2 * at[b], s2)]
        for k in range(AXES[b] - 1):
            total = total + in2[m, k * s2 : (k + 1) * s2]
        sum2[m, 0:s2] = total
        mine = pl.ds(at[d] * s2, s2)
        in3[m, mine] = total
        flying[m] = go([copy(sum2.at[m, pl.ds(0, s2)], in3.at[m, mine], peer(d, k)) for k in range(1, AXES[d])])

    def gather2(m):
        a, b, d, s, s2 = sizes(m)
        landed(m)
        total = in3[m, 0:s2]
        for j in range(1, AXES[d]):
            total = total + in3[m, j * s2 : (j + 1) * s2]
        spot = pl.ds(m * PER_MODE + first + s * at[a] + s2 * at[b], s2)
        probe_sum[spot] = total * scale
        block = probe_sum.at[spot]
        flying[m] = go([copy(block, block, peer(b, k)) for k in range(1, AXES[b])])

    def gather1(m):
        a, _, _, s, _ = sizes(m)
        landed(m)
        block = probe_sum.at[pl.ds(m * PER_MODE + first + s * at[a], s)]
        flying[m] = go([copy(block, block, peer(a, k)) for k in range(1, AXES[a])])

    def gather0(m):
        landed(m)
        block = probe_sum.at[pl.ds(m * PER_MODE + first, PART)]
        flying[m] = go([copy(block, block, twin)])

    chain = (swap, reduce1, reduce2, reduce3, gather2, gather1, gather0, landed)
    done = [0] * M

    def advance(*modes):
        for m in modes:
            if done[m] < len(chain):
                chain[done[m]](m)
                done[m] += 1

    for m in range(M):
        backward(m, probe, fwd, bwd, patch, rows_in, cols_in, wave, terms, pacc)
        advance(*range(max(0, m - 1), m + 1))

    def put(slot, carry):
        place(slot, corners, terms, spread)
        return carry

    lax.fori_loop(0, SLOTS, put, 0)
    advance(3, 0)

    def into(ref):
        def store(k, row, j, value):
            ref[k, pl.ds(row, 8), 128 * j : 128 * j + 128] = value

        return store

    n_cols = E // 128
    bands = (lo, hi, mid)
    strips = [lo, hi] + [pl.ds(RIM + 128 * i, 128) for i in range(T // 128)]
    pass_down = relayed(way_down, [(g_down.at[:, :, b], passing2.at[:, :, b], above.at[:, :, b]) for b in strips])
    pass_up = relayed(way_up, [(g_up.at[:, :, b], passing2.at[:, :, b], below.at[:, :, b]) for b in strips])
    every = range(len(strips))
    gather(corners, spread, 0, RIM, range(n_cols), into(g_up))
    f_up = [copy(g_up.at[:, :, b], below.at[:, :, b], to_up) for b in bands]
    go(f_up, up_direct)
    pass_up[0](*every)
    gather(corners, spread, RIM + T, RIM, range(n_cols), into(g_down))
    f_down = [copy(g_down.at[:, :, b], above.at[:, :, b], to_down) for b in bands]
    go(f_down, down_direct)
    pass_down[0](*every)
    gather(corners, spread, RIM, T, (0,), into(g_left))
    gather(corners, spread, RIM, T, (n_cols - 1,), into(g_right))
    parts = (pl.ds(RIM, T - 2 * RIM), pl.ds(0, RIM), pl.ds(T - RIM, RIM))
    f_left = [copy(g_left.at[:, p, :], right_in.at[:, p, :], to_left) for p in parts]
    f_right = [copy(g_right.at[:, p, :], left_in.at[:, p, :], to_right) for p in parts]
    go(f_left[:1], left)
    go(f_right[:1], right)
    advance(1)
    for i in (0, 1):
        pass_down[1](i)
        pass_up[1](i)
    advance(0, 2)
    pass_down[1](2)
    pass_up[1](2)

    for i in range(2):
        arrived(above_direct, f_down[i], way_down, pass_down, (i,))

    @pl.when(up)
    def _():
        g_left[:, 0:RIM, :] += above[:, :, 0:RIM]
        g_right[:, 0:RIM, :] += above[:, :, RIM + T :]

    go(f_left[1:2], left)
    go(f_right[1:2], right)
    for i in range(2):
        arrived(below_direct, f_up[i], way_up, pass_up, (i,))

    @pl.when(down)
    def _():
        g_left[:, T - RIM :, :] += below[:, :, 0:RIM]
        g_right[:, T - RIM :, :] += below[:, :, RIM + T :]

    go(f_left[2:], left)
    go(f_right[2:], right)
    for i in every[3:]:
        pass_down[1](i)
        pass_up[1](i)
    advance(1, 3, 2)
    gather(corners, spread, RIM, T, range(1, n_cols - 1), into(core_sum))
    advance(0, 3, 1, 0, 2, 1)
    arrived(above_direct, f_down[2], way_down, pass_down, every[2:])

    @pl.when(up)
    def _():
        core_sum[:, 0:RIM, :] += above[:, :, RIM : RIM + T]

    arrived(below_direct, f_up[2], way_up, pass_up, every[2:])

    @pl.when(down)
    def _():
        core_sum[:, T - RIM :, :] += below[:, :, RIM : RIM + T]

    advance(3, 2, 0, 3, 1)

    @pl.when(left)
    def _():
        for one in f_right:
            one.wait_recv()
        core_sum[:, :, 0:RIM] += left_in[...]

    @pl.when(right)
    def _():
        for one in f_left:
            one.wait_recv()
        core_sum[:, :, T - RIM :] += right_in[...]

    stores = [pltpu.make_async_copy(core_sum, core_out, load_sem.at[0])]
    stores[0].start()
    advance(2, 3)
    for m in range(M):
        advance(m)
        whole = pl.ds(m * PER_MODE, PER_MODE)
        stores.append(pltpu.make_async_copy(probe_sum.at[whole], probe_out.at[whole], load_sem.at[m + 1]))
        stores[-1].start()
    for one in stores:
        one.wait()
    for there, some in sent:
        if there is None:
            for one in some:
                one.wait_send()
        else:

            @pl.when(there)
            def _(some=some):
                for one in some:
                    one.wait_send()


def on_device(object_field, probe, photons, positions, live_counts):
    fwd = dft_table(S)
    f32, bf16 = jnp.float32, jnp.bfloat16
    tile = object_field.reshape(2, T // 8, 8, T // 128, 128).transpose(0, 1, 3, 2, 4)
    smem, anywhere = (pl.BlockSpec(memory_space=m) for m in (pltpu.SMEM, pl.ANY))
    core, probe_grad = pl.pallas_call(
        kernel,
        out_shape=(
            jax.ShapeDtypeStruct((2, T, T), f32),
            jax.ShapeDtypeStruct((GROUPS, 8, S), f32),
        ),
        in_specs=[smem, smem, anywhere, anywhere, anywhere, anywhere, anywhere],
        out_specs=(anywhere, anywhere),
        scratch_shapes=[
            pltpu.VMEM((2, ROWS, COLS, 8, 128), f32),
            pltpu.VMEM((M, 2, S, S), f32),
            pltpu.VMEM((SLOTS, S, S), jnp.int32),
            pltpu.VMEM((2 * S, 2 * S), bf16),
            pltpu.VMEM((2 * S, 2 * S), bf16),
            pltpu.VMEM((SLOTS, 2, S, S), f32),
            pltpu.VMEM((SLOTS, M, 2 * S, S), bf16),
            pltpu.VMEM((M, S, 2 * S), bf16),
            pltpu.VMEM((M, S, 2 * S), f32),
            pltpu.VMEM((SLOTS, 2, S, S), f32),
            pltpu.VMEM((SLOTS, 2, WROWS + 2, WCOLS + 2, 8, 128), f32),
            pltpu.VMEM((GROUPS, 8, S), f32),
            pltpu.VMEM((2, RIM, E), f32),
            pltpu.VMEM((2, RIM, E), f32),
            pltpu.VMEM((2, T, RIM), f32),
            pltpu.VMEM((2, T, RIM), f32),
            pltpu.VMEM((2, RIM, E), f32),
            pltpu.VMEM((2, RIM, E), f32),
            pltpu.VMEM((2, T, RIM), f32),
            pltpu.VMEM((2, T, RIM), f32),
            pltpu.VMEM((GROUPS // 2, 8, S), f32),
            pltpu.VMEM((GROUPS // 2, 8, S), f32),
            pltpu.VMEM((M, PART, 8, S), f32),
            pltpu.VMEM((M, PART // 4, 8, S), f32),
            pltpu.VMEM((M, PART // 2, 8, S), f32),
            pltpu.VMEM((M, PART // 4, 8, S), f32),
            pltpu.VMEM((M, PART // 16, 8, S), f32),
            pltpu.VMEM((2, RIM // 8, E // 128, 8, 128), f32),
            pltpu.VMEM((2, RIM, E), f32),
            pltpu.VMEM((2, T, T), f32),
            pltpu.VMEM((GROUPS, 8, S), f32),
            pltpu.SemaphoreType.DMA((N_COPIES,)),
            pltpu.SemaphoreType.DMA((N_COPIES,)),
            pltpu.SemaphoreType.DMA((5,)),
        ],
        compiler_params=pltpu.CompilerParams(collective_id=0, has_side_effects=True, vmem_limit_bytes=60 << 20),
    )(positions[0, 0].T, live_counts, tile, probe, photons[0, 0], fwd, fwd.T.copy())
    return core, probe_grad.reshape(M, 2, S, S)


def solution(mesh):
    in_specs = (
        P(None, "rows", "cols"),
        P(),
        P("rows", "cols", None, None, None),
        P("rows", "cols", None, None),
        P("rows", "cols"),
    )
    out_specs = (P(None, "rows", "cols"), P())
    return jax.shard_map(on_device, mesh=mesh, in_specs=in_specs, out_specs=out_specs, check_vma=False)
```

```python
import math

import jax
import jax.numpy as jnp
import numpy as np
from jax import lax
from jax.experimental import pallas as pl
from jax.experimental.pallas import tpu as pltpu
from jax.sharding import PartitionSpec as P

MESH = pl.DeviceIdType.MESH
background = 1.0
S = 256
RIM = 128
T = 512
E = T + 2 * RIM
M = 4
SLOTS = 4
WROWS, WCOLS = S // 8 + 1, S // 128 + 1
ROWS, COLS = E // 8 + 1, E // 128 + 1
STEP = 32
GROUPS = M * 2 * S // 8
PER_MODE = GROUPS // M
PART = PER_MODE // 2
AXES = {"x": 4, "y": 4, "z": 8}
ORDERS = (("y", "x", "z"), ("x", "y", "z"), ("y", "x", "z"), ("x", "y", "z"))
N_SUM = sum(2 + 2 * (AXES[a] - 1) + 2 * (AXES[b] - 1) + AXES[d] - 1 for a, b, d in ORDERS)
N_COPIES = 24 + 48 + N_SUM


def dft_table(wave_size):
    ramp = np.arange(wave_size, dtype=np.int32)
    phases = ramp[:, None] * ramp[None, :] % wave_size
    angles = phases.astype(np.float32) * np.float32(2.0 * math.pi / wave_size)
    scaling = np.float32(1.0 / math.sqrt(wave_size))
    cos_t = (np.cos(angles) * scaling).astype(jnp.bfloat16)
    sin_t = (np.sin(angles) * scaling).astype(jnp.bfloat16)
    return np.block([[cos_t, sin_t], [-sin_t, cos_t]])


def dot(a, b):
    return jnp.dot(a, b, preferred_element_type=jnp.float32)


def box(corners, slot):
    top, left = corners[0, slot] + RIM, corners[1, slot] + RIM
    shift = lax.shift_right_logical
    return shift(top, 3), shift(left, 7), lax.bitwise_and(top, 7), lax.bitwise_and(left, 127)


def forward(slot, corners, live, padded, probe, counts, fwd, bwd, patch, rows_in, cols_in, wave):
    lane = lax.broadcasted_iota(jnp.int32, (8, 128), 1)
    sublane = lax.broadcasted_iota(jnp.int32, (8, 128), 0)
    top0, left0, down, over = box(corners, slot)
    back_by, up_by = lax.bitwise_and(128 - over, 127), lax.bitwise_and(8 - down, 7)
    keep = lane < 128 - over
    for k in range(2):
        before = None
        for i in range(WROWS):
            a, b, d = (pltpu.roll(padded[k, top0 + i, left0 + j], back_by, 1) for j in range(3))
            now = tuple(pltpu.roll(v, up_by, 0) for v in (jnp.where(keep, a, b), jnp.where(keep, b, d)))
            if i:
                for j in range(2):
                    patch[slot, k, 8 * i - 8 : 8 * i, 128 * j : 128 * j + 128] = jnp.where(
                        sublane < 8 - down, before[j], now[j]
                    )
            before = now
    for m in range(M):
        for r in range(0, S, STEP):
            here = pl.ds(r, STEP)
            o_re, o_im = patch[slot, 0, here, :], patch[slot, 1, here, :]
            p_re, p_im = probe[m, 0, here, :], probe[m, 1, here, :]
            rows_in[slot, m, r : r + STEP, :] = (p_re * o_re - p_im * o_im).astype(jnp.bfloat16)
            rows_in[slot, m, S + r : S + r + STEP, :] = (p_re * o_im + p_im * o_re).astype(jnp.bfloat16)
        half = dot(fwd[...], rows_in[slot, m])
        cols_in[m, :, 0:S] = half[0:S].astype(jnp.bfloat16)
        cols_in[m, :, S:] = half[S:].astype(jnp.bfloat16)
        wave[m] = dot(cols_in[m], bwd[...])
    alive = jnp.full((STEP, S), live[0, 0]) > slot
    for r in range(0, S, STEP):
        here = pl.ds(r, STEP)
        total = None
        for m in range(M):
            w_re, w_im = wave[m, here, 0:S], wave[m, here, S:]
            term = w_re * w_re + w_im * w_im
            total = term if m == 0 else total + term
        factor = 1.0 - counts[slot, here, :].astype(jnp.float32) / (total + background)
        factor = jnp.where(alive, factor, 0.0)
        for m in range(M):
            rows_in[slot, m, r : r + STEP, :] = (factor * wave[m, here, 0:S]).astype(jnp.bfloat16)
            rows_in[slot, m, S + r : S + r + STEP, :] = (factor * wave[m, here, S:]).astype(jnp.bfloat16)


def backward(m, probe, fwd, bwd, patch, rows_in, cols_in, wave, terms, pacc):
    for slot in range(SLOTS):
        back = dot(bwd[...], rows_in[slot, m])
        cols_in[slot, :, 0:S] = back[0:S].astype(jnp.bfloat16)
        cols_in[slot, :, S:] = back[S:].astype(jnp.bfloat16)
        wave[slot] = dot(cols_in[slot], fwd[...])
    for r in range(0, S, STEP):
        here = pl.ds(r, STEP)
        p_re, p_im = probe[m, 0, here, :], probe[m, 1, here, :]
        q_re = q_im = None
        for slot in range(SLOTS):
            c_re, c_im = wave[slot, here, 0:S], wave[slot, here, S:]
            o_re, o_im = patch[slot, 0, here, :], patch[slot, 1, here, :]
            a_re, a_im = p_re * c_re + p_im * c_im, p_re * c_im - p_im * c_re
            if m:
                a_re, a_im = terms[slot, 0, here, :] + a_re, terms[slot, 1, here, :] + a_im
            terms[slot, 0, here, :], terms[slot, 1, here, :] = a_re, a_im
            b_re, b_im = o_re * c_re + o_im * c_im, o_re * c_im - o_im * c_re
            q_re, q_im = (b_re, b_im) if slot == 0 else (q_re + b_re, q_im + b_im)
        for i in range(STEP // 8):
            g = m * PER_MODE + r // 8 + i
            pacc[g] = q_re[8 * i : 8 * i + 8]
            pacc[g + PART] = q_im[8 * i : 8 * i + 8]


def place(slot, corners, terms, spread):
    lane = lax.broadcasted_iota(jnp.int32, (8, 128), 1)
    sublane = lax.broadcasted_iota(jnp.int32, (8, 128), 0)
    nothing = jnp.zeros((8, 128), jnp.float32)
    _, _, down, over = box(corners, slot)
    ahead_by, down_by = lax.bitwise_and(over, 127), lax.bitwise_and(down, 7)
    inside = lane >= over
    for k in range(2):
        before = (nothing, nothing)
        for i in range(WROWS):
            now = (nothing, nothing)
            if i < S // 8:
                now = tuple(
                    pltpu.roll(terms[slot, k, 8 * i : 8 * i + 8, 128 * j : 128 * j + 128], down_by, 0) for j in range(2)
                )
            a, b = (pltpu.roll(jnp.where(sublane >= down, now[j], before[j]), ahead_by, 1) for j in range(2))
            before = now
            for j, v in enumerate((jnp.where(inside, a, 0.0), jnp.where(inside, b, a), jnp.where(inside, 0.0, b))):
                spread[slot, k, i + 1, j + 1] = v


def gather(corners, spread, row0, rows, cols, store):
    places = [box(corners, slot)[:2] for slot in range(SLOTS)]
    at_col = [[lax.max(lax.min(c - left0, WCOLS), -1) + 1 for c in cols] for _, left0 in places]

    def body(i, carry):
        at_row = [lax.max(lax.min(row0 // 8 + i - top0, WROWS), -1) + 1 for top0, _ in places]
        for j in range(len(cols)):
            for k in range(2):
                value = None
                for slot in range(SLOTS):
                    one = spread[slot, k, at_row[slot], at_col[slot][j]]
                    value = one if slot == 0 else value + one
                store(k, pl.multiple_of(8 * i, 8), j, value)
        return carry

    lax.fori_loop(0, rows // 8, body, 0, unroll=2)


def kernel(
    corners, live, tile, probe_hbm, photons, fwd_hbm, bwd_hbm, core_out, left_out, right_out, probe_out,
    padded, probe, counts, fwd, bwd, patch, rows_in, cols_in, wave, terms, spread, pacc,
    g_up, g_down, g_left, g_right, above, below, left_in, right_in, from_twin, acc,
    in1, in2, in3, sum1, sum2, passing, passing2, core_sum, probe_sum, send_sem, recv_sem, load_sem,
):
    r, c = lax.axis_index("rows"), lax.axis_index("cols")
    n_r, n_c = lax.axis_size("rows"), lax.axis_size("cols")
    up, down, left, right = r > 0, r < n_r - 1, c > 0, c < n_c - 1
    to_up, to_down, to_left, to_right = (r - 1, c), (r + 1, c), (r, c - 1), (r, c + 1)
    sides = ((up, to_up), (down, to_down), (left, to_left), (right, to_right))
    core = r % 2
    at = {"x": r // 16 * 2 + c // 4, "y": c % 4, "z": r // 2 % 8}
    twin = (r + 1 - 2 * core, c)

    def peer(axis, k):
        spot = dict(at)
        spot[axis] = (at[axis] + k) % AXES[axis]
        return (spot["x"] // 2 * 16 + spot["z"] * 2 + core, spot["x"] % 2 * 4 + spot["y"])

    lo, mid, hi = pl.ds(0, RIM), pl.ds(RIM, T), pl.ds(RIM + T, RIM)
    r_lo, r_mid, r_hi = pl.ds(0, RIM // 8), pl.ds(RIM // 8, T // 8), pl.ds((RIM + T) // 8, RIM // 8)
    c_lo, c_mid, c_hi = pl.ds(0, 1), pl.ds(1, T // 128), pl.ds(1 + T // 128, 1)
    loads = [
        pltpu.make_async_copy(src, dst, load_sem.at[i])
        for i, (src, dst) in enumerate(
            ((tile, padded.at[:, r_mid, c_mid]), (probe_hbm, probe), (fwd_hbm, fwd), (bwd_hbm, bwd), (photons, counts))
        )
    ]
    loads[0].start()
    n_half, middle = n_r // 2, (c == n_c // 2 - 1) | (c == n_c // 2)
    at_corner, past = (c == 0) | (c == n_c - 1), jnp.where(c < n_c // 2, n_c - 1, 0)
    back = jnp.where(c == 0, n_c // 2, n_c // 2 - 1)
    way_down = ((r == n_half - 1) & middle, (n_r - 1, past), (r == n_r - 1) & at_corner, (n_half - 1, back), (n_half, back), (r == n_half) & middle)
    way_up = ((r == n_half) & middle, (0, past), (r == 0) & at_corner, (n_half, back), (n_half - 1, back), (r == n_half - 1) & middle)
    ways = (way_down, way_up)
    peers = [twin] + [peer(axis, k) for axis in AXES for k in range(1, AXES[axis])]
    barrier = pltpu.get_barrier_semaphore()
    for there, device in sides:

        @pl.when(there)
        def _(device=device):
            pl.semaphore_signal(barrier, inc=1, device_id=device, device_id_type=MESH)

    for source, relay, is_relay, from_device, _, target in ways:

        @pl.when(is_relay)
        def _(device=from_device):
            pl.semaphore_signal(barrier, inc=1, device_id=device, device_id_type=MESH)

        @pl.when(target)
        def _(device=relay):
            pl.semaphore_signal(barrier, inc=1, device_id=device, device_id_type=MESH)

    for device in peers:
        pl.semaphore_signal(barrier, inc=1, device_id=device, device_id_type=MESH)
    for one in loads[1:]:
        one.start()
    loads[0].wait()
    pl.semaphore_wait(barrier, len(peers) + sum(jnp.where(there, 1, 0) for there, _ in sides) + sum(jnp.where(way[0], 1, 0) + jnp.where(way[2], 1, 0) for way in ways))

    count = [0]

    def copy(src, dst, device):
        index = count[0]
        count[0] += 1
        return pltpu.make_async_remote_copy(
            src_ref=src,
            dst_ref=dst,
            send_sem=send_sem.at[index],
            recv_sem=recv_sem.at[index],
            device_id=device,
            device_id_type=MESH,
        )

    sent = []

    def go(some, there=None):
        if there is None:
            for one in some:
                one.start()
        else:

            @pl.when(there)
            def _():
                for one in some:
                    one.start()

        sent.append((there, some))
        return some

    def relayed(way, pieces):
        legs = [(copy(src, buf, way[1]), copy(buf, dst, way[4])) for src, buf, dst in pieces]

        def depart(*some):
            go([legs[i][0] for i in some], way[0])

        def pass_on(*some):
            for i in some:

                @pl.when(way[2])
                def _(i=i):
                    legs[i][0].wait_recv()

                go([legs[i][1]], way[2])

        def arrive(*some):
            for i in some:
                legs[i][1].wait_recv()

        return depart, pass_on, arrive

    down_direct, up_direct = down & jnp.logical_not(way_down[0]), up & jnp.logical_not(way_up[0])
    above_direct, below_direct = up & jnp.logical_not(way_down[5]), down & jnp.logical_not(way_up[5])

    r_near, r_far = pl.ds(RIM // 8, RIM // 8), pl.ds(T // 8, RIM // 8)
    c_near, c_far = pl.ds(1, 1), pl.ds(T // 128, 1)
    spans = (r_near, r_far, pl.ds(2 * RIM // 8, (T - 2 * RIM) // 8))
    to_l = [copy(padded.at[:, s, c_near], padded.at[:, s, c_hi], to_left) for s in spans]
    to_r = [copy(padded.at[:, s, c_far], padded.at[:, s, c_lo], to_right) for s in spans]
    to_u = copy(padded.at[:, r_near, c_mid], padded.at[:, r_hi, c_mid], to_up)
    to_d = copy(padded.at[:, r_far, c_mid], padded.at[:, r_lo, c_mid], to_down)
    c_ul = copy(padded.at[:, r_near, c_lo], padded.at[:, r_hi, c_lo], to_up)
    c_ur = copy(padded.at[:, r_near, c_hi], padded.at[:, r_hi, c_hi], to_up)
    c_dl = copy(padded.at[:, r_far, c_lo], padded.at[:, r_lo, c_lo], to_down)
    c_dr = copy(padded.at[:, r_far, c_hi], padded.at[:, r_lo, c_hi], to_down)
    blocks = [pl.ds(1 + i, 1) for i in range(T // 128)] + [c_lo, c_hi]
    strips_in = range(T // 128)
    relay_down = relayed(way_down, [(padded.at[:, r_far, b], passing.at[:, :, b], padded.at[:, r_lo, b]) for b in blocks])
    relay_up = relayed(way_up, [(padded.at[:, r_near, b], passing.at[:, :, b], padded.at[:, r_hi, b]) for b in blocks])
    for i in range(3):
        go([to_l[i]], left)
        go([to_r[i]], right)
        if i == 0:
            go([to_u], up_direct)
            go([to_d], down_direct)
            relay_down[0](*strips_in)
            relay_up[0](*strips_in)

    for slot in range(SLOTS):
        spread[slot, :, 0] = jnp.zeros((2, WCOLS + 2, 8, 128), jnp.float32)
        spread[slot, :, WROWS + 1] = jnp.zeros((2, WCOLS + 2, 8, 128), jnp.float32)
        spread[slot, :, :, 0] = jnp.zeros((2, WROWS + 2, 8, 128), jnp.float32)
        spread[slot, :, :, WCOLS + 1] = jnp.zeros((2, WROWS + 2, 8, 128), jnp.float32)
    padded[:, ROWS - 1] = jnp.zeros((2, COLS, 8, 128), jnp.float32)
    padded[:, :, COLS - 1] = jnp.zeros((2, ROWS, 8, 128), jnp.float32)

    def zeroed(there, rows, cols):
        @pl.when(jnp.logical_not(there))
        def _():
            padded[:, rows, cols] = jnp.zeros((2, rows.size, cols.size, 8, 128), jnp.float32)

    def arrived(there, one, way=None, relay=None, some=()):
        @pl.when(there)
        def _():
            one.wait_recv()

        if way is not None:

            @pl.when(way[5])
            def _():
                relay[2](*some)

    for there, rows, cols in (
        (left, r_mid, c_lo), (right, r_mid, c_hi), (up, r_lo, c_mid), (down, r_hi, c_mid),
        (up & left, r_lo, c_lo), (up & right, r_lo, c_hi), (down & left, r_hi, c_lo), (down & right, r_hi, c_hi),
    ):
        zeroed(there, rows, cols)
    corner_l, corner_r = len(blocks) - 2, len(blocks) - 1
    relay_down[1](*strips_in)
    relay_up[1](*strips_in)
    arrived(left, to_r[0])
    go([c_ul], left & up_direct)
    relay_up[0](corner_l)
    arrived(right, to_l[0])
    go([c_ur], right & up_direct)
    relay_up[0](corner_r)
    arrived(left, to_r[1])
    go([c_dl], left & down_direct)
    relay_down[0](corner_l)
    arrived(right, to_l[1])
    go([c_dr], right & down_direct)
    relay_down[0](corner_r)
    for i in (corner_l, corner_r):
        relay_down[1](i)
        relay_up[1](i)
    arrived(above_direct, to_d, way_down, relay_down, strips_in)
    arrived(below_direct, to_u, way_up, relay_up, strips_in)
    arrived(left, to_r[2])
    arrived(right, to_l[2])
    arrived(above_direct & left, c_dl, way_down, relay_down, (corner_l,))
    arrived(above_direct & right, c_dr, way_down, relay_down, (corner_r,))
    arrived(below_direct & left, c_ul, way_up, relay_up, (corner_l,))
    arrived(below_direct & right, c_ur, way_up, relay_up, (corner_r,))
    for one in loads[1:]:
        one.wait()

    def visit(slot, carry):
        forward(slot, corners, live, padded, probe, counts, fwd, bwd, patch, rows_in, cols_in, wave)
        return carry

    lax.fori_loop(0, SLOTS, visit, 0)

    first, other = PART * core, PART * (1 - core)
    flying = {}

    def sizes(m):
        a, b, d = ORDERS[m]
        return a, b, d, PART // AXES[a], PART // AXES[a] // AXES[b]

    def swap(m):
        src = pacc.at[pl.ds(m * PER_MODE + other, PART)]
        flying[m] = go([copy(src, from_twin.at[pl.ds(m * PART, PART)], twin)])

    def landed(m):
        for one in flying[m]:
            one.wait_recv()

    def reduce1(m):
        a, _, _, s, _ = sizes(m)
        landed(m)
        here = pl.ds(m * PART, PART)
        acc[here] = pacc[pl.ds(m * PER_MODE + first, PART)] + from_twin[here]
        flying[m] = go(
            [
                copy(
                    acc.at[pl.ds(m * PART + s * ((at[a] + k) % AXES[a]), s)],
                    in1.at[m, pl.ds((k - 1) * s, s)],
                    peer(a, k),
                )
                for k in range(1, AXES[a])
            ]
        )

    def reduce2(m):
        a, b, _, s, s2 = sizes(m)
        landed(m)
        total = acc[pl.ds(m * PART + s * at[a], s)]
        for k in range(AXES[a] - 1):
            total = total + in1[m, k * s : (k + 1) * s]
        sum1[m, 0:s] = total
        flying[m] = go(
            [
                copy(
                    sum1.at[m, pl.ds(s2 * ((at[b] + k) % AXES[b]), s2)],
                    in2.at[m, pl.ds((k - 1) * s2, s2)],
                    peer(b, k),
                )
                for k in range(1, AXES[b])
            ]
        )

    def reduce3(m):
        _, b, d, _, s2 = sizes(m)
        landed(m)
        total = sum1[m, pl.ds(s2 * at[b], s2)]
        for k in range(AXES[b] - 1):
            total = total + in2[m, k * s2 : (k + 1) * s2]
        sum2[m, 0:s2] = total
        mine = pl.ds(at[d] * s2, s2)
        in3[m, mine] = total
        flying[m] = go([copy(sum2.at[m, pl.ds(0, s2)], in3.at[m, mine], peer(d, k)) for k in range(1, AXES[d])])

    def gather2(m):
        a, b, d, s, s2 = sizes(m)
        landed(m)
        total = in3[m, 0:s2]
        for j in range(1, AXES[d]):
            total = total + in3[m, j * s2 : (j + 1) * s2]
        spot = pl.ds(m * PER_MODE + first + s * at[a] + s2 * at[b], s2)
        probe_sum[spot] = total
        block = probe_sum.at[spot]
        flying[m] = go([copy(block, block, peer(b, k)) for k in range(1, AXES[b])])

    def gather1(m):
        a, _, _, s, _ = sizes(m)
        landed(m)
        block = probe_sum.at[pl.ds(m * PER_MODE + first + s * at[a], s)]
        flying[m] = go([copy(block, block, peer(a, k)) for k in range(1, AXES[a])])

    def gather0(m):
        landed(m)
        block = probe_sum.at[pl.ds(m * PER_MODE + first, PART)]
        flying[m] = go([copy(block, block, twin)])

    chain = (swap, reduce1, reduce2, reduce3, gather2, gather1, gather0, landed)
    done = [0] * M

    def advance(*modes):
        for m in modes:
            if done[m] < len(chain):
                chain[done[m]](m)
                done[m] += 1

    for m in range(M):
        backward(m, probe, fwd, bwd, patch, rows_in, cols_in, wave, terms, pacc)
        advance(*range(max(0, m - 1), m + 1))

    def put(slot, carry):
        place(slot, corners, terms, spread)
        return carry

    lax.fori_loop(0, SLOTS // 2, put, 0)
    advance(3)
    lax.fori_loop(SLOTS // 2, SLOTS, put, 0)
    advance(0)

    def into(ref):
        def store(k, row, j, value):
            ref[k, pl.ds(row, 8), 128 * j : 128 * j + 128] = value

        return store

    n_cols = E // 128
    bands = (lo, hi, mid)
    strips = [lo, hi] + [pl.ds(RIM + 128 * i, 128) for i in range(T // 128)]
    pass_down = relayed(way_down, [(g_down.at[:, :, b], passing2.at[:, :, b], above.at[:, :, b]) for b in strips])
    pass_up = relayed(way_up, [(g_up.at[:, :, b], passing2.at[:, :, b], below.at[:, :, b]) for b in strips])
    every = range(len(strips))
    gather(corners, spread, 0, RIM, range(n_cols), into(g_up))
    f_up = [copy(g_up.at[:, :, b], below.at[:, :, b], to_up) for b in bands]
    go(f_up, up_direct)
    pass_up[0](*every)
    gather(corners, spread, RIM + T, RIM, range(n_cols), into(g_down))
    f_down = [copy(g_down.at[:, :, b], above.at[:, :, b], to_down) for b in bands]
    go(f_down, down_direct)
    pass_down[0](*every)
    gather(corners, spread, RIM, T, (0,), into(g_left))
    gather(corners, spread, RIM, T, (n_cols - 1,), into(g_right))
    parts = (pl.ds(RIM, T - 2 * RIM), pl.ds(0, RIM), pl.ds(T - RIM, RIM))
    f_left = [copy(g_left.at[:, p, :], right_in.at[:, p, :], to_left) for p in parts]
    f_right = [copy(g_right.at[:, p, :], left_in.at[:, p, :], to_right) for p in parts]
    go(f_left[:1], left)
    go(f_right[:1], right)
    advance(1, 0, 2, 3)
    for i in (0, 1):
        pass_down[1](i)
        pass_up[1](i)

    for i in range(2):
        arrived(above_direct, f_down[i], way_down, pass_down, (i,))

    @pl.when(up)
    def _():
        g_left[:, 0:RIM, :] += above[:, :, 0:RIM]
        g_right[:, 0:RIM, :] += above[:, :, RIM + T :]

    go(f_left[1:2], left)
    go(f_right[1:2], right)
    for i in range(2):
        arrived(below_direct, f_up[i], way_up, pass_up, (i,))

    @pl.when(down)
    def _():
        g_left[:, T - RIM :, :] += below[:, :, 0:RIM]
        g_right[:, T - RIM :, :] += below[:, :, RIM + T :]

    go(f_left[2:], left)
    go(f_right[2:], right)
    advance(1, 2)
    for i in every[2:]:
        pass_down[1](i)
        pass_up[1](i)
    advance(3)
    gather(corners, spread, RIM, T, range(1, n_cols - 1), into(core_sum))
    advance(0, 1, 2, 3, 0, 1, 2)
    arrived(above_direct, f_down[2], way_down, pass_down, every[2:])

    @pl.when(up)
    def _():
        core_sum[:, 0:RIM, :] += above[:, :, RIM : RIM + T]

    arrived(below_direct, f_up[2], way_up, pass_up, every[2:])

    @pl.when(down)
    def _():
        core_sum[:, T - RIM :, :] += below[:, :, RIM : RIM + T]

    stores = [pltpu.make_async_copy(core_sum, core_out, load_sem.at[0])]
    stores[0].start()
    advance(3, 0, 1, 2)
    for there, some, ref, out in ((left, f_right, left_in, left_out), (right, f_left, right_in, right_out)):

        @pl.when(there)
        def _(some=some):
            for one in some:
                one.wait_recv()

        @pl.when(jnp.logical_not(there))
        def _(ref=ref):
            ref[...] = jnp.zeros_like(ref)

        stores.append(pltpu.make_async_copy(ref, out, load_sem.at[len(stores)]))
        stores[-1].start()
    advance(3)
    for m in range(M):
        advance(m)
        whole = pl.ds(m * PER_MODE, PER_MODE)
        stores.append(pltpu.make_async_copy(probe_sum.at[whole], probe_out.at[whole], load_sem.at[len(stores)]))
        stores[-1].start()
    for one in stores:
        one.wait()

    for there, some in sent:
        if there is None:
            for one in some:
                one.wait_send()
        else:

            @pl.when(there)
            def _(some=some):
                for one in some:
                    one.wait_send()


def on_device(object_field, probe, photons, positions, live_counts):
    fwd = dft_table(S)
    f32, bf16 = jnp.float32, jnp.bfloat16
    tile = object_field.reshape(2, T // 8, 8, T // 128, 128).transpose(0, 1, 3, 2, 4)
    smem, anywhere = (pl.BlockSpec(memory_space=m) for m in (pltpu.SMEM, pl.ANY))
    core, left, right, probe_total = pl.pallas_call(
        kernel,
        out_shape=(
            jax.ShapeDtypeStruct((2, T, T), f32),
            jax.ShapeDtypeStruct((2, T, RIM), f32),
            jax.ShapeDtypeStruct((2, T, RIM), f32),
            jax.ShapeDtypeStruct((GROUPS, 8, S), f32),
        ),
        in_specs=[smem, smem, anywhere, anywhere, anywhere, anywhere, anywhere],
        out_specs=(anywhere,) * 4,
        scratch_shapes=[
            pltpu.VMEM((2, ROWS, COLS, 8, 128), f32),
            pltpu.VMEM((M, 2, S, S), f32),
            pltpu.VMEM((SLOTS, S, S), jnp.int32),
            pltpu.VMEM((2 * S, 2 * S), bf16),
            pltpu.VMEM((2 * S, 2 * S), bf16),
            pltpu.VMEM((SLOTS, 2, S, S), f32),
            pltpu.VMEM((SLOTS, M, 2 * S, S), bf16),
            pltpu.VMEM((M, S, 2 * S), bf16),
            pltpu.VMEM((M, S, 2 * S), f32),
            pltpu.VMEM((SLOTS, 2, S, S), f32),
            pltpu.VMEM((SLOTS, 2, WROWS + 2, WCOLS + 2, 8, 128), f32),
            pltpu.VMEM((GROUPS, 8, S), f32),
            pltpu.VMEM((2, RIM, E), f32),
            pltpu.VMEM((2, RIM, E), f32),
            pltpu.VMEM((2, T, RIM), f32),
            pltpu.VMEM((2, T, RIM), f32),
            pltpu.VMEM((2, RIM, E), f32),
            pltpu.VMEM((2, RIM, E), f32),
            pltpu.VMEM((2, T, RIM), f32),
            pltpu.VMEM((2, T, RIM), f32),
            pltpu.VMEM((GROUPS // 2, 8, S), f32),
            pltpu.VMEM((GROUPS // 2, 8, S), f32),
            pltpu.VMEM((M, PART, 8, S), f32),
            pltpu.VMEM((M, PART // 4, 8, S), f32),
            pltpu.VMEM((M, PART // 2, 8, S), f32),
            pltpu.VMEM((M, PART // 4, 8, S), f32),
            pltpu.VMEM((M, PART // 16, 8, S), f32),
            pltpu.VMEM((2, RIM // 8, E // 128, 8, 128), f32),
            pltpu.VMEM((2, RIM, E), f32),
            pltpu.VMEM((2, T, T), f32),
            pltpu.VMEM((GROUPS, 8, S), f32),
            pltpu.SemaphoreType.DMA((N_COPIES,)),
            pltpu.SemaphoreType.DMA((N_COPIES,)),
            pltpu.SemaphoreType.DMA((3 + M,)),
        ],
        compiler_params=pltpu.CompilerParams(collective_id=0, has_side_effects=True, vmem_limit_bytes=60 << 20),
    )(positions[0, 0].T, live_counts, tile, probe, photons[0, 0], fwd, fwd.T.copy())
    keep = ((0, 0), (0, 0))
    object_grad = core + jnp.pad(left, (*keep, (0, T - RIM))) + jnp.pad(right, (*keep, (T - RIM, 0)))
    probe_grad = probe_total.reshape(M, 2, S, S) / math.sqrt(lax.axis_size("rows") * lax.axis_size("cols"))
    return object_grad, probe_grad


def solution(mesh):
    in_specs = (
        P(None, "rows", "cols"),
        P(),
        P("rows", "cols", None, None, None),
        P("rows", "cols", None, None),
        P("rows", "cols"),
    )
    out_specs = (P(None, "rows", "cols"), P())
    return jax.shard_map(on_device, mesh=mesh, in_specs=in_specs, out_specs=out_specs, check_vma=False)
```

```python
import math

import jax
import jax.numpy as jnp
import numpy as np
from jax import lax
from jax.experimental import pallas as pl
from jax.experimental.pallas import tpu as pltpu
from jax.sharding import PartitionSpec as P

MESH = pl.DeviceIdType.MESH
background = 1.0
S = 256
RIM = 128
T = 512
E = T + 2 * RIM
M = 4
SLOTS = 4
WROWS, WCOLS = S // 8 + 1, S // 128 + 1
ROWS, COLS = E // 8 + 1, E // 128 + 1
STEP = 32
GROUPS = M * 2 * S // 8
PER_MODE = GROUPS // M
PART = PER_MODE // 2
AXES = {"x": 4, "y": 4, "z": 8}
ORDERS = (("y", "x", "z"), ("x", "y", "z"), ("y", "x", "z"), ("x", "y", "z"))
N_SUM = sum(2 + 2 * (AXES[a] - 1) + 2 * (AXES[b] - 1) + AXES[d] - 1 for a, b, d in ORDERS)
N_COPIES = 24 + 48 + N_SUM


def dft_table(wave_size):
    ramp = np.arange(wave_size, dtype=np.int32)
    phases = ramp[:, None] * ramp[None, :] % wave_size
    angles = phases.astype(np.float32) * np.float32(2.0 * math.pi / wave_size)
    scaling = np.float32(1.0 / math.sqrt(wave_size))
    cos_t = (np.cos(angles) * scaling).astype(jnp.bfloat16)
    sin_t = (np.sin(angles) * scaling).astype(jnp.bfloat16)
    return np.block([[cos_t, sin_t], [-sin_t, cos_t]])


def dot(a, b):
    return jnp.dot(a, b, preferred_element_type=jnp.float32)


def box(corners, slot):
    top, left = corners[0, slot] + RIM, corners[1, slot] + RIM
    shift = lax.shift_right_logical
    return shift(top, 3), shift(left, 7), lax.bitwise_and(top, 7), lax.bitwise_and(left, 127)


def forward(slot, corners, live, padded, probe, counts, fwd, bwd, patch, rows_in, cols_in, wave):
    lane = lax.broadcasted_iota(jnp.int32, (8, 128), 1)
    sublane = lax.broadcasted_iota(jnp.int32, (8, 128), 0)
    top0, left0, down, over = box(corners, slot)
    back_by, up_by = lax.bitwise_and(128 - over, 127), lax.bitwise_and(8 - down, 7)
    keep = lane < 128 - over
    for k in range(2):
        before = None
        for i in range(WROWS):
            a, b, d = (pltpu.roll(padded[k, top0 + i, left0 + j], back_by, 1) for j in range(3))
            now = tuple(pltpu.roll(v, up_by, 0) for v in (jnp.where(keep, a, b), jnp.where(keep, b, d)))
            if i:
                for j in range(2):
                    patch[slot, k, 8 * i - 8 : 8 * i, 128 * j : 128 * j + 128] = jnp.where(
                        sublane < 8 - down, before[j], now[j]
                    )
            before = now
    for m in range(M):
        for r in range(0, S, STEP):
            here = pl.ds(r, STEP)
            o_re, o_im = patch[slot, 0, here, :], patch[slot, 1, here, :]
            p_re, p_im = probe[m, 0, here, :], probe[m, 1, here, :]
            rows_in[slot, m, r : r + STEP, :] = (p_re * o_re - p_im * o_im).astype(jnp.bfloat16)
            rows_in[slot, m, S + r : S + r + STEP, :] = (p_re * o_im + p_im * o_re).astype(jnp.bfloat16)
        half = dot(fwd[...], rows_in[slot, m])
        cols_in[m, :, 0:S] = half[0:S].astype(jnp.bfloat16)
        cols_in[m, :, S:] = half[S:].astype(jnp.bfloat16)
        wave[m] = dot(cols_in[m], bwd[...])
    alive = jnp.full((STEP, S), live[0, 0]) > slot
    for r in range(0, S, STEP):
        here = pl.ds(r, STEP)
        total = None
        for m in range(M):
            w_re, w_im = wave[m, here, 0:S], wave[m, here, S:]
            term = w_re * w_re + w_im * w_im
            total = term if m == 0 else total + term
        factor = 1.0 - counts[slot, here, :].astype(jnp.float32) / (total + background)
        factor = jnp.where(alive, factor, 0.0)
        for m in range(M):
            rows_in[slot, m, r : r + STEP, :] = (factor * wave[m, here, 0:S]).astype(jnp.bfloat16)
            rows_in[slot, m, S + r : S + r + STEP, :] = (factor * wave[m, here, S:]).astype(jnp.bfloat16)


def backward(m, probe, fwd, bwd, patch, rows_in, cols_in, wave, terms, pacc):
    for slot in range(SLOTS):
        back = dot(bwd[...], rows_in[slot, m])
        cols_in[slot, :, 0:S] = back[0:S].astype(jnp.bfloat16)
        cols_in[slot, :, S:] = back[S:].astype(jnp.bfloat16)
        wave[slot] = dot(cols_in[slot], fwd[...])
    for r in range(0, S, STEP):
        here = pl.ds(r, STEP)
        p_re, p_im = probe[m, 0, here, :], probe[m, 1, here, :]
        q_re = q_im = None
        for slot in range(SLOTS):
            c_re, c_im = wave[slot, here, 0:S], wave[slot, here, S:]
            o_re, o_im = patch[slot, 0, here, :], patch[slot, 1, here, :]
            a_re, a_im = p_re * c_re + p_im * c_im, p_re * c_im - p_im * c_re
            if m:
                a_re, a_im = terms[slot, 0, here, :] + a_re, terms[slot, 1, here, :] + a_im
            terms[slot, 0, here, :], terms[slot, 1, here, :] = a_re, a_im
            b_re, b_im = o_re * c_re + o_im * c_im, o_re * c_im - o_im * c_re
            q_re, q_im = (b_re, b_im) if slot == 0 else (q_re + b_re, q_im + b_im)
        for i in range(STEP // 8):
            g = m * PER_MODE + r // 8 + i
            pacc[g] = q_re[8 * i : 8 * i + 8]
            pacc[g + PART] = q_im[8 * i : 8 * i + 8]


def place(slot, corners, terms, spread):
    lane = lax.broadcasted_iota(jnp.int32, (8, 128), 1)
    sublane = lax.broadcasted_iota(jnp.int32, (8, 128), 0)
    nothing = jnp.zeros((8, 128), jnp.float32)
    _, _, down, over = box(corners, slot)
    ahead_by, down_by = lax.bitwise_and(over, 127), lax.bitwise_and(down, 7)
    inside = lane >= over
    for k in range(2):
        before = (nothing, nothing)
        for i in range(WROWS):
            now = (nothing, nothing)
            if i < S // 8:
                now = tuple(
                    pltpu.roll(terms[slot, k, 8 * i : 8 * i + 8, 128 * j : 128 * j + 128], down_by, 0) for j in range(2)
                )
            a, b = (pltpu.roll(jnp.where(sublane >= down, now[j], before[j]), ahead_by, 1) for j in range(2))
            before = now
            for j, v in enumerate((jnp.where(inside, a, 0.0), jnp.where(inside, b, a), jnp.where(inside, 0.0, b))):
                spread[slot, k, i + 1, j + 1] = v


def gather(corners, spread, row0, rows, cols, store):
    places = [box(corners, slot)[:2] for slot in range(SLOTS)]
    at_col = [[lax.max(lax.min(c - left0, WCOLS), -1) + 1 for c in cols] for _, left0 in places]

    def body(i, carry):
        at_row = [lax.max(lax.min(row0 // 8 + i - top0, WROWS), -1) + 1 for top0, _ in places]
        for j in range(len(cols)):
            for k in range(2):
                value = None
                for slot in range(SLOTS):
                    one = spread[slot, k, at_row[slot], at_col[slot][j]]
                    value = one if slot == 0 else value + one
                store(k, pl.multiple_of(8 * i, 8), j, value)
        return carry

    lax.fori_loop(0, rows // 8, body, 0, unroll=2)


def kernel(
    corners, live, tile, probe_hbm, photons, fwd_hbm, bwd_hbm, core_out, left_out, right_out, probe_out,
    padded, probe, counts, fwd, bwd, patch, rows_in, cols_in, wave, terms, spread, pacc,
    g_up, g_down, g_left, g_right, above, below, left_in, right_in, from_twin, acc,
    in1, in2, in3, sum1, sum2, passing, passing2, core_sum, probe_sum, send_sem, recv_sem, load_sem,
):
    r, c = lax.axis_index("rows"), lax.axis_index("cols")
    n_r, n_c = lax.axis_size("rows"), lax.axis_size("cols")
    up, down, left, right = r > 0, r < n_r - 1, c > 0, c < n_c - 1
    to_up, to_down, to_left, to_right = (r - 1, c), (r + 1, c), (r, c - 1), (r, c + 1)
    sides = ((up, to_up), (down, to_down), (left, to_left), (right, to_right))
    core = r % 2
    at = {"x": r // 16 * 2 + c // 4, "y": c % 4, "z": r // 2 % 8}
    twin = (r + 1 - 2 * core, c)

    def peer(axis, k):
        spot = dict(at)
        spot[axis] = (at[axis] + k) % AXES[axis]
        return (spot["x"] // 2 * 16 + spot["z"] * 2 + core, spot["x"] % 2 * 4 + spot["y"])

    lo, mid, hi = pl.ds(0, RIM), pl.ds(RIM, T), pl.ds(RIM + T, RIM)
    r_lo, r_mid, r_hi = pl.ds(0, RIM // 8), pl.ds(RIM // 8, T // 8), pl.ds((RIM + T) // 8, RIM // 8)
    c_lo, c_mid, c_hi = pl.ds(0, 1), pl.ds(1, T // 128), pl.ds(1 + T // 128, 1)
    loads = [
        pltpu.make_async_copy(src, dst, load_sem.at[i])
        for i, (src, dst) in enumerate(
            ((tile, padded.at[:, r_mid, c_mid]), (probe_hbm, probe), (fwd_hbm, fwd), (bwd_hbm, bwd), (photons, counts))
        )
    ]
    loads[0].start()
    n_half, middle = n_r // 2, (c == n_c // 2 - 1) | (c == n_c // 2)
    at_corner, past = (c == 0) | (c == n_c - 1), jnp.where(c < n_c // 2, n_c - 1, 0)
    back = jnp.where(c == 0, n_c // 2, n_c // 2 - 1)
    way_down = ((r == n_half - 1) & middle, (n_r - 1, past), (r == n_r - 1) & at_corner, (n_half - 1, back), (n_half, back), (r == n_half) & middle)
    way_up = ((r == n_half) & middle, (0, past), (r == 0) & at_corner, (n_half, back), (n_half - 1, back), (r == n_half - 1) & middle)
    ways = (way_down, way_up)
    peers = [twin] + [peer(axis, k) for axis in AXES for k in range(1, AXES[axis])]
    barrier = pltpu.get_barrier_semaphore()
    for there, device in sides:

        @pl.when(there)
        def _(device=device):
            pl.semaphore_signal(barrier, inc=1, device_id=device, device_id_type=MESH)

    for source, relay, is_relay, from_device, _, target in ways:

        @pl.when(is_relay)
        def _(device=from_device):
            pl.semaphore_signal(barrier, inc=1, device_id=device, device_id_type=MESH)

        @pl.when(target)
        def _(device=relay):
            pl.semaphore_signal(barrier, inc=1, device_id=device, device_id_type=MESH)

    for device in peers:
        pl.semaphore_signal(barrier, inc=1, device_id=device, device_id_type=MESH)
    for one in loads[1:]:
        one.start()
    loads[0].wait()
    pl.semaphore_wait(barrier, len(peers) + sum(jnp.where(there, 1, 0) for there, _ in sides) + sum(jnp.where(way[0], 1, 0) + jnp.where(way[2], 1, 0) for way in ways))

    count = [0]

    def copy(src, dst, device):
        index = count[0]
        count[0] += 1
        return pltpu.make_async_remote_copy(
            src_ref=src,
            dst_ref=dst,
            send_sem=send_sem.at[index],
            recv_sem=recv_sem.at[index],
            device_id=device,
            device_id_type=MESH,
        )

    sent = []

    def go(some, there=None):
        if there is None:
            for one in some:
                one.start()
        else:

            @pl.when(there)
            def _():
                for one in some:
                    one.start()

        sent.append((there, some))
        return some

    def relayed(way, pieces):
        legs = [(copy(src, buf, way[1]), copy(buf, dst, way[4])) for src, buf, dst in pieces]

        def depart(*some):
            go([legs[i][0] for i in some], way[0])

        def pass_on(*some):
            for i in some:

                @pl.when(way[2])
                def _(i=i):
                    legs[i][0].wait_recv()

                go([legs[i][1]], way[2])

        def arrive(*some):
            for i in some:
                legs[i][1].wait_recv()

        return depart, pass_on, arrive

    down_direct, up_direct = down & jnp.logical_not(way_down[0]), up & jnp.logical_not(way_up[0])
    above_direct, below_direct = up & jnp.logical_not(way_down[5]), down & jnp.logical_not(way_up[5])

    r_near, r_far = pl.ds(RIM // 8, RIM // 8), pl.ds(T // 8, RIM // 8)
    c_near, c_far = pl.ds(1, 1), pl.ds(T // 128, 1)
    spans = (r_near, r_far, pl.ds(2 * RIM // 8, (T - 2 * RIM) // 8))
    to_l = [copy(padded.at[:, s, c_near], padded.at[:, s, c_hi], to_left) for s in spans]
    to_r = [copy(padded.at[:, s, c_far], padded.at[:, s, c_lo], to_right) for s in spans]
    to_u = copy(padded.at[:, r_near, c_mid], padded.at[:, r_hi, c_mid], to_up)
    to_d = copy(padded.at[:, r_far, c_mid], padded.at[:, r_lo, c_mid], to_down)
    c_ul = copy(padded.at[:, r_near, c_lo], padded.at[:, r_hi, c_lo], to_up)
    c_ur = copy(padded.at[:, r_near, c_hi], padded.at[:, r_hi, c_hi], to_up)
    c_dl = copy(padded.at[:, r_far, c_lo], padded.at[:, r_lo, c_lo], to_down)
    c_dr = copy(padded.at[:, r_far, c_hi], padded.at[:, r_lo, c_hi], to_down)
    blocks = [pl.ds(1 + i, 1) for i in range(T // 128)] + [c_lo, c_hi]
    strips_in = range(T // 128)
    relay_down = relayed(way_down, [(padded.at[:, r_far, b], passing.at[:, :, b], padded.at[:, r_lo, b]) for b in blocks])
    relay_up = relayed(way_up, [(padded.at[:, r_near, b], passing.at[:, :, b], padded.at[:, r_hi, b]) for b in blocks])
    for i in range(3):
        go([to_l[i]], left)
        go([to_r[i]], right)
        if i == 0:
            go([to_u], up_direct)
            go([to_d], down_direct)
            relay_down[0](*strips_in)
            relay_up[0](*strips_in)

    for slot in range(SLOTS):
        spread[slot, :, 0] = jnp.zeros((2, WCOLS + 2, 8, 128), jnp.float32)
        spread[slot, :, WROWS + 1] = jnp.zeros((2, WCOLS + 2, 8, 128), jnp.float32)
        spread[slot, :, :, 0] = jnp.zeros((2, WROWS + 2, 8, 128), jnp.float32)
        spread[slot, :, :, WCOLS + 1] = jnp.zeros((2, WROWS + 2, 8, 128), jnp.float32)
    padded[:, ROWS - 1] = jnp.zeros((2, COLS, 8, 128), jnp.float32)
    padded[:, :, COLS - 1] = jnp.zeros((2, ROWS, 8, 128), jnp.float32)

    def zeroed(there, rows, cols):
        @pl.when(jnp.logical_not(there))
        def _():
            padded[:, rows, cols] = jnp.zeros((2, rows.size, cols.size, 8, 128), jnp.float32)

    def arrived(there, one, way=None, relay=None, some=()):
        @pl.when(there)
        def _():
            one.wait_recv()

        if way is not None:

            @pl.when(way[5])
            def _():
                relay[2](*some)

    for there, rows, cols in (
        (left, r_mid, c_lo), (right, r_mid, c_hi), (up, r_lo, c_mid), (down, r_hi, c_mid),
        (up & left, r_lo, c_lo), (up & right, r_lo, c_hi), (down & left, r_hi, c_lo), (down & right, r_hi, c_hi),
    ):
        zeroed(there, rows, cols)
    corner_l, corner_r = len(blocks) - 2, len(blocks) - 1
    relay_down[1](*strips_in)
    relay_up[1](*strips_in)
    arrived(left, to_r[0])
    go([c_ul], left & up_direct)
    relay_up[0](corner_l)
    arrived(right, to_l[0])
    go([c_ur], right & up_direct)
    relay_up[0](corner_r)
    arrived(left, to_r[1])
    go([c_dl], left & down_direct)
    relay_down[0](corner_l)
    arrived(right, to_l[1])
    go([c_dr], right & down_direct)
    relay_down[0](corner_r)
    for i in (corner_l, corner_r):
        relay_down[1](i)
        relay_up[1](i)
    arrived(above_direct, to_d, way_down, relay_down, strips_in)
    arrived(below_direct, to_u, way_up, relay_up, strips_in)
    arrived(left, to_r[2])
    arrived(right, to_l[2])
    arrived(above_direct & left, c_dl, way_down, relay_down, (corner_l,))
    arrived(above_direct & right, c_dr, way_down, relay_down, (corner_r,))
    arrived(below_direct & left, c_ul, way_up, relay_up, (corner_l,))
    arrived(below_direct & right, c_ur, way_up, relay_up, (corner_r,))
    for one in loads[1:]:
        one.wait()

    def visit(slot, carry):
        forward(slot, corners, live, padded, probe, counts, fwd, bwd, patch, rows_in, cols_in, wave)
        return carry

    lax.fori_loop(0, SLOTS, visit, 0)

    first, other = PART * core, PART * (1 - core)
    flying = {}

    def sizes(m):
        a, b, d = ORDERS[m]
        return a, b, d, PART // AXES[a], PART // AXES[a] // AXES[b]

    def swap(m):
        src = pacc.at[pl.ds(m * PER_MODE + other, PART)]
        flying[m] = go([copy(src, from_twin.at[pl.ds(m * PART, PART)], twin)])

    def landed(m):
        for one in flying[m]:
            one.wait_recv()

    def reduce1(m):
        a, _, _, s, _ = sizes(m)
        landed(m)
        here = pl.ds(m * PART, PART)
        acc[here] = pacc[pl.ds(m * PER_MODE + first, PART)] + from_twin[here]
        flying[m] = go(
            [
                copy(
                    acc.at[pl.ds(m * PART + s * ((at[a] + k) % AXES[a]), s)],
                    in1.at[m, pl.ds((k - 1) * s, s)],
                    peer(a, k),
                )
                for k in range(1, AXES[a])
            ]
        )

    def reduce2(m):
        a, b, _, s, s2 = sizes(m)
        landed(m)
        total = acc[pl.ds(m * PART + s * at[a], s)]
        for k in range(AXES[a] - 1):
            total = total + in1[m, k * s : (k + 1) * s]
        sum1[m, 0:s] = total
        flying[m] = go(
            [
                copy(
                    sum1.at[m, pl.ds(s2 * ((at[b] + k) % AXES[b]), s2)],
                    in2.at[m, pl.ds((k - 1) * s2, s2)],
                    peer(b, k),
                )
                for k in range(1, AXES[b])
            ]
        )

    def reduce3(m):
        _, b, d, _, s2 = sizes(m)
        landed(m)
        total = sum1[m, pl.ds(s2 * at[b], s2)]
        for k in range(AXES[b] - 1):
            total = total + in2[m, k * s2 : (k + 1) * s2]
        sum2[m, 0:s2] = total
        mine = pl.ds(at[d] * s2, s2)
        in3[m, mine] = total
        flying[m] = go([copy(sum2.at[m, pl.ds(0, s2)], in3.at[m, mine], peer(d, k)) for k in range(1, AXES[d])])

    def gather2(m):
        a, b, d, s, s2 = sizes(m)
        landed(m)
        total = in3[m, 0:s2]
        for j in range(1, AXES[d]):
            total = total + in3[m, j * s2 : (j + 1) * s2]
        spot = pl.ds(m * PER_MODE + first + s * at[a] + s2 * at[b], s2)
        probe_sum[spot] = total
        block = probe_sum.at[spot]
        flying[m] = go([copy(block, block, peer(b, k)) for k in range(1, AXES[b])])

    def gather1(m):
        a, _, _, s, _ = sizes(m)
        landed(m)
        block = probe_sum.at[pl.ds(m * PER_MODE + first + s * at[a], s)]
        flying[m] = go([copy(block, block, peer(a, k)) for k in range(1, AXES[a])])

    def gather0(m):
        landed(m)
        block = probe_sum.at[pl.ds(m * PER_MODE + first, PART)]
        flying[m] = go([copy(block, block, twin)])

    chain = (swap, reduce1, reduce2, reduce3, gather2, gather1, gather0, landed)
    done = [0] * M

    def advance(*modes):
        for m in modes:
            if done[m] < len(chain):
                chain[done[m]](m)
                done[m] += 1

    for m in range(M):
        backward(m, probe, fwd, bwd, patch, rows_in, cols_in, wave, terms, pacc)
        advance(*range(max(0, m - 1), m + 1))

    def put(slot, carry):
        place(slot, corners, terms, spread)
        return carry

    lax.fori_loop(0, SLOTS // 2, put, 0)
    advance(3)
    lax.fori_loop(SLOTS // 2, SLOTS, put, 0)
    advance(0)

    def into(ref):
        def store(k, row, j, value):
            ref[k, pl.ds(row, 8), 128 * j : 128 * j + 128] = value

        return store

    n_cols = E // 128
    bands = (lo, hi, mid)
    strips = [lo, hi] + [pl.ds(RIM + 128 * i, 128) for i in range(T // 128)]
    pass_down = relayed(way_down, [(g_down.at[:, :, b], passing2.at[:, :, b], above.at[:, :, b]) for b in strips])
    pass_up = relayed(way_up, [(g_up.at[:, :, b], passing2.at[:, :, b], below.at[:, :, b]) for b in strips])
    every = range(len(strips))
    gather(corners, spread, 0, RIM, range(n_cols), into(g_up))
    f_up = [copy(g_up.at[:, :, b], below.at[:, :, b], to_up) for b in bands]
    go(f_up, up_direct)
    pass_up[0](*every)
    gather(corners, spread, RIM + T, RIM, range(n_cols), into(g_down))
    f_down = [copy(g_down.at[:, :, b], above.at[:, :, b], to_down) for b in bands]
    go(f_down, down_direct)
    pass_down[0](*every)
    gather(corners, spread, RIM, T, (0,), into(g_left))
    gather(corners, spread, RIM, T, (n_cols - 1,), into(g_right))
    parts = (pl.ds(RIM, T - 2 * RIM), pl.ds(0, RIM), pl.ds(T - RIM, RIM))
    f_left = [copy(g_left.at[:, p, :], right_in.at[:, p, :], to_left) for p in parts]
    f_right = [copy(g_right.at[:, p, :], left_in.at[:, p, :], to_right) for p in parts]
    go(f_left[:1], left)
    go(f_right[:1], right)
    advance(1, 0, 2, 3)
    for i in (0, 1):
        pass_down[1](i)
        pass_up[1](i)

    for i in range(2):
        arrived(above_direct, f_down[i], way_down, pass_down, (i,))

    @pl.when(up)
    def _():
        g_left[:, 0:RIM, :] += above[:, :, 0:RIM]
        g_right[:, 0:RIM, :] += above[:, :, RIM + T :]

    go(f_left[1:2], left)
    go(f_right[1:2], right)
    for i in range(2):
        arrived(below_direct, f_up[i], way_up, pass_up, (i,))

    @pl.when(down)
    def _():
        g_left[:, T - RIM :, :] += below[:, :, 0:RIM]
        g_right[:, T - RIM :, :] += below[:, :, RIM + T :]

    go(f_left[2:], left)
    go(f_right[2:], right)
    advance(1, 2)
    for i in every[2:]:
        pass_down[1](i)
        pass_up[1](i)
    advance(3)
    gather(corners, spread, RIM, T, range(1, n_cols - 1), into(core_sum))
    advance(0, 1, 2, 3, 0, 1, 2)
    arrived(above_direct, f_down[2], way_down, pass_down, every[2:])

    @pl.when(up)
    def _():
        core_sum[:, 0:RIM, :] += above[:, :, RIM : RIM + T]

    arrived(below_direct, f_up[2], way_up, pass_up, every[2:])

    @pl.when(down)
    def _():
        core_sum[:, T - RIM :, :] += below[:, :, RIM : RIM + T]

    stores = [pltpu.make_async_copy(core_sum, core_out, load_sem.at[0])]
    stores[0].start()
    advance(3, 0, 1, 2)
    for there, some, ref, out in ((left, f_right, left_in, left_out), (right, f_left, right_in, right_out)):

        @pl.when(there)
        def _(some=some):
            for one in some:
                one.wait_recv()

        @pl.when(jnp.logical_not(there))
        def _(ref=ref):
            ref[...] = jnp.zeros_like(ref)

        stores.append(pltpu.make_async_copy(ref, out, load_sem.at[len(stores)]))
        stores[-1].start()
    advance(3)
    for m in range(M):
        advance(m)
        whole = pl.ds(m * PER_MODE, PER_MODE)
        stores.append(pltpu.make_async_copy(probe_sum.at[whole], probe_out.at[whole], load_sem.at[len(stores)]))
        stores[-1].start()
    for one in stores:
        one.wait()

    for there, some in sent:
        if there is None:
            for one in some:
                one.wait_send()
        else:

            @pl.when(there)
            def _(some=some):
                for one in some:
                    one.wait_send()


def on_device(object_field, probe, photons, positions, live_counts):
    fwd = dft_table(S)
    f32, bf16 = jnp.float32, jnp.bfloat16
    tile = object_field.reshape(2, T // 8, 8, T // 128, 128).transpose(0, 1, 3, 2, 4)
    smem, anywhere = (pl.BlockSpec(memory_space=m) for m in (pltpu.SMEM, pl.ANY))
    core, left, right, probe_total = pl.pallas_call(
        kernel,
        out_shape=(
            jax.ShapeDtypeStruct((2, T, T), f32),
            jax.ShapeDtypeStruct((2, T, RIM), f32),
            jax.ShapeDtypeStruct((2, T, RIM), f32),
            jax.ShapeDtypeStruct((GROUPS, 8, S), f32),
        ),
        in_specs=[smem, smem, anywhere, anywhere, anywhere, anywhere, anywhere],
        out_specs=(anywhere,) * 4,
        scratch_shapes=[
            pltpu.VMEM((2, ROWS, COLS, 8, 128), f32),
            pltpu.VMEM((M, 2, S, S), f32),
            pltpu.VMEM((SLOTS, S, S), jnp.int32),
            pltpu.VMEM((2 * S, 2 * S), bf16),
            pltpu.VMEM((2 * S, 2 * S), bf16),
            pltpu.VMEM((SLOTS, 2, S, S), f32),
            pltpu.VMEM((SLOTS, M, 2 * S, S), bf16),
            pltpu.VMEM((M, S, 2 * S), bf16),
            pltpu.VMEM((M, S, 2 * S), f32),
            pltpu.VMEM((SLOTS, 2, S, S), f32),
            pltpu.VMEM((SLOTS, 2, WROWS + 2, WCOLS + 2, 8, 128), f32),
            pltpu.VMEM((GROUPS, 8, S), f32),
            pltpu.VMEM((2, RIM, E), f32),
            pltpu.VMEM((2, RIM, E), f32),
            pltpu.VMEM((2, T, RIM), f32),
            pltpu.VMEM((2, T, RIM), f32),
            pltpu.VMEM((2, RIM, E), f32),
            pltpu.VMEM((2, RIM, E), f32),
            pltpu.VMEM((2, T, RIM), f32),
            pltpu.VMEM((2, T, RIM), f32),
            pltpu.VMEM((GROUPS // 2, 8, S), f32),
            pltpu.VMEM((GROUPS // 2, 8, S), f32),
            pltpu.VMEM((M, PART, 8, S), f32),
            pltpu.VMEM((M, PART // 4, 8, S), f32),
            pltpu.VMEM((M, PART // 2, 8, S), f32),
            pltpu.VMEM((M, PART // 4, 8, S), f32),
            pltpu.VMEM((M, PART // 16, 8, S), f32),
            pltpu.VMEM((2, RIM // 8, E // 128, 8, 128), f32),
            pltpu.VMEM((2, RIM, E), f32),
            pltpu.VMEM((2, T, T), f32),
            pltpu.VMEM((GROUPS, 8, S), f32),
            pltpu.SemaphoreType.DMA((N_COPIES,)),
            pltpu.SemaphoreType.DMA((N_COPIES,)),
            pltpu.SemaphoreType.DMA((3 + M,)),
        ],
        compiler_params=pltpu.CompilerParams(collective_id=0, has_side_effects=True, vmem_limit_bytes=60 << 20),
    )(positions[0, 0].T, live_counts, tile, probe, photons[0, 0], fwd, fwd.T.copy())
    object_grad = jnp.concatenate(
        [core[:, :, :RIM] + left, core[:, :, RIM : T - RIM], core[:, :, T - RIM :] + right], axis=2
    )
    probe_grad = probe_total.reshape(M, 2, S, S) / math.sqrt(lax.axis_size("rows") * lax.axis_size("cols"))
    return object_grad, probe_grad


def solution(mesh):
    in_specs = (
        P(None, "rows", "cols"),
        P(),
        P("rows", "cols", None, None, None),
        P("rows", "cols", None, None),
        P("rows", "cols"),
    )
    out_specs = (P(None, "rows", "cols"), P())
    return jax.shard_map(on_device, mesh=mesh, in_specs=in_specs, out_specs=out_specs, check_vma=False)
```
